32 devices in a mesh: groups: 2 (over y), pool: 4 (over z), tp: 2 (over x), pair: 2 (over core).
Axes of the slice: x: 2, y: 2, z: 4, core: 2. Of those that a mesh axis runs over, the one named last changes fastest.
Arguments:
- tokens: bfloat16 [2048, 4096], P(('groups', 'pool', 'pair'), 'tp'), parts along dimension 0, may hold values from -6 to 6
- routes: int32 [2048, 8], P(('groups', 'pool', 'pair')), parts along dimension 0, may hold values from 0 to 127, as said below
- gate_weights: int32 [2048, 8], P(('groups', 'pool', 'pair')), parts along dimension 0, may hold values from 1 to 255
- w_gate: bfloat16 [8, 4096, 1024], P(('pool', 'pair'), None, 'tp'), may hold values from -0.09375 to 0.09375
- w_up: bfloat16 [8, 4096, 1024], P(('pool', 'pair'), None, 'tp'), may hold values from -0.09375 to 0.09375
- w_down: bfloat16 [8, 1024, 4096], P(('pool', 'pair'), 'tp'), may hold values from -0.75 to 0.75
Outputs:
- mixed: bfloat16 [2048, 4096], P(('groups', 'pool', 'pair'), 'tp'), parts along dimension 0
The draws below stay inside these ranges and needn't reach their ends.
There are 2 independent parts, one for each index of `groups`. The reference program is written for one: setup_inputs(seed, part) draws one part's arguments, and reference() takes and returns one part's arrays. A program takes and returns all parts, laid end to end along the dimension named above; an argument that names none is the same for every part. Nothing has to cross between parts.
Inputs may be any that keep to these rules, and one draw needn't show every extreme that they name: `routes`: each row names 8 different experts; within the rows of one index of pool and pair (aligned blocks of 128 rows) no expert is named by more than 16 rows.
All inputs are finite; a program needn't handle non-finite values.
Results may differ from the reference program's by a relative error of at most 0.0085.
Values may be sent and summed in bfloat16 or wider, within the bound.
No kernel may reach another device: no remote copies, remote signals or barrier semaphores. Data moves between devices by JAX's collectives and lax.ppermute only.
A program may use at most 64 MiB of HBM per device.

```python
import jax
import jax.numpy as jnp
from jax import lax

D = 4096
FFE = 1024
EXPERTS = 128
TOPK = 8
TOK_DEV = 128
FLIGHT = 8
CAP = 16
TOKENS = 1024
N_POOL = 4
N_TP = 2
N_PAIR = 2


def draw_routes(key, part):
    key = jax.random.fold_in(key, 11)
    base = TOK_DEV * TOPK // EXPERTS
    hot = jax.random.randint(jax.random.fold_in(key, 1), (), 0, FLIGHT)
    blocks = TOKENS // TOK_DEV
    keys = jax.random.split(jax.random.fold_in(key, 2), blocks)

    def one_block(block_key):
        k_load, k_label, k_order = jax.random.split(block_key, 3)
        moved = jax.random.randint(k_load, (EXPERTS // 2,), 0, base + 1)
        moved = moved.at[0].set(base)
        loads = jnp.stack([base + moved, base - moved], axis=1).reshape(EXPERTS)
        labels = jax.random.permutation(k_label, EXPERTS).astype(jnp.int32)
        spot = jnp.argmax(labels == hot)
        labels = labels.at[spot].set(labels[0]).at[0].set(hot)
        ends = jnp.cumsum(loads)
        position = jnp.arange(TOK_DEV * TOPK)
        owner = jnp.sum((ends[None, :] <= position[:, None]).astype(jnp.int32), axis=1)
        picks = labels[owner].reshape(TOPK, TOK_DEV).T
        order = jax.random.permutation(k_order, TOK_DEV)
        return picks[order]
    return jax.vmap(one_block)(keys).reshape(TOKENS, TOPK).astype(jnp.int32)


def with_ends(entries, own_key, smallest, high):
    longest = entries.shape.index(max(entries.shape))
    spots = []
    for shift in (0, 1):
        where = [jax.random.randint(jax.random.fold_in(own_key, axis), (), 0, length) for axis, length in enumerate(entries.shape)]
        where[longest] = (where[longest] + shift) % entries.shape[longest]
        spots.append(tuple(where))
    return entries.at[spots[0]].set(smallest).at[spots[1]].set(high)


def block_scale(stream_key, dims, shards, smallest, top_value):
    loudness = 1.0
    for dim, blocks in shards:
        draws = jax.random.uniform(jax.random.fold_in(jax.random.fold_in(stream_key, 6), dim), (blocks,), jnp.float32, smallest / len(shards), top_value / len(shards))
        loudness = loudness * jnp.repeat(jnp.exp(draws), dims[dim] // blocks).reshape((-1,) + (1,) * (len(dims) - 1 - dim))
    return loudness


def centred(stream_key, dims, scale, reach, shards=(), kind=jnp.bfloat16):
    result = scale * jax.random.normal(stream_key, dims, jnp.float32)
    if shards:
        result = result * block_scale(stream_key, dims, shards, -0.22, 0.18)
    return jnp.clip(result, -reach, reach).astype(kind)


def setup_inputs(seed: int = 0, part: int = 0) -> dict:
    arg_keys = jax.random.split(jax.random.key(seed), 7)
    part_keys = jax.random.split(jax.random.fold_in(arg_keys[6], part), 7)
    return {
        "tokens": centred(part_keys[0], (TOKENS, D), 1.0, 6.0, ((0, 8), (1, 2))),
        "routes": draw_routes(jax.random.fold_in(jax.random.fold_in(arg_keys[6], part), 71), part),
        "gate_weights": with_ends(jax.random.randint(part_keys[2], (TOKENS, TOPK), 1, 256), jax.random.fold_in(part_keys[2], 1), 1, 255).astype(jnp.int32),
        "w_gate": centred(arg_keys[3], (FLIGHT, D, FFE), D ** -0.5, 0.09375, ((0, 8), (2, 2))),
        "w_up": centred(arg_keys[4], (FLIGHT, D, FFE), D ** -0.5, 0.09375, ((0, 8), (2, 2))),
        "w_down": centred(arg_keys[5], (FLIGHT, FFE, D), (FFE // 16) ** -0.5, 0.75, ((0, 8), (1, 2))),
    }


def expert_rows(rows, gate_w, up_w, down_w):
    hp = lax.Precision.HIGHEST
    x = rows.astype(jnp.float32)
    gate = jnp.dot(x, gate_w.astype(jnp.float32), precision=hp)
    up = jnp.dot(x, up_w.astype(jnp.float32), precision=hp)
    hidden = (jax.nn.silu(gate) * up).astype(jnp.bfloat16)
    width = hidden.shape[1] // N_TP
    blocks = hidden.astype(jnp.float32).reshape(hidden.shape[0], N_TP, width)
    down = down_w.astype(jnp.float32).reshape(N_TP, width, down_w.shape[1])
    parts = jnp.einsum("ntf,tfd->ntd", blocks, down, precision=hp)
    rounded = lax.optimization_barrier(parts.astype(jnp.bfloat16))
    return jnp.sum(rounded.astype(jnp.float32), axis=1).astype(jnp.bfloat16)


def reference(tokens, routes, gate_weights, w_gate, w_up, w_down):
    flight = N_POOL * N_PAIR
    slots = flight * CAP
    totals = jnp.sum(gate_weights, axis=1).astype(jnp.float32)
    share_all = gate_weights.astype(jnp.float32) / totals[:, None]

    def one(carry, expert):
        match = routes == expert
        hit = jnp.any(match, axis=1)
        share = jnp.sum(jnp.where(match, share_all, 0.0), axis=1)
        index = jnp.nonzero(hit, size=slots, fill_value=0)[0].astype(jnp.int32)
        valid = jnp.arange(slots, dtype=jnp.int32) < jnp.sum(hit.astype(jnp.int32))
        rows = tokens[index]
        out = expert_rows(rows, w_gate[expert], w_up[expert], w_down[expert])
        weight = jnp.where(valid, share[index], 0.0)
        carry = carry.at[index].add(weight[:, None] * out.astype(jnp.float32))
        return carry, None

    start = jnp.zeros(tokens.shape, jnp.float32)
    total, _ = lax.scan(one, start, jnp.arange(flight, dtype=jnp.int32))
    return total.astype(jnp.bfloat16)
```

```python
import functools

import jax
import jax.numpy as jnp
from jax import lax
from jax.experimental import pallas as pl
from jax.experimental.pallas import tpu as pltpu
from jax.sharding import PartitionSpec as P

CAP = 16
VMEM = pl.BlockSpec(memory_space=pltpu.VMEM)
SMEM = pl.BlockSpec(memory_space=pltpu.SMEM)
PARAMS = pltpu.CompilerParams(vmem_limit_bytes=24 * 2**20)
BF16, F32 = jnp.bfloat16, jnp.float32


def picks(routes_t, experts):
    hits = [
        jnp.max((routes_t == e).astype(F32), axis=0, keepdims=True) for e in experts
    ]
    hits = jnp.concatenate(hits, axis=0)
    streams = hits.shape[1]
    earlier = lax.broadcasted_iota(jnp.int32, (streams, streams), 0)
    later = lax.broadcasted_iota(jnp.int32, (streams, streams), 1)
    before = (earlier < later).astype(BF16)
    slots = jnp.dot(hits.astype(BF16), before, preferred_element_type=F32)
    return hits, slots


def one_hot(hits, slots, row):
    streams = hits.shape[1]
    slot = lax.broadcasted_iota(jnp.int32, (CAP, streams), 0).astype(F32)
    return jnp.where((slots[row : row + 1] == slot) & (hits[row : row + 1] > 0), 1.0, 0.0)


def select_kernel(n_pool, n_pair, chunks, pos_ref, *refs):
    tokens, routes, outs = refs[:n_pair], refs[n_pair : 2 * n_pair], refs[2 * n_pair :]
    pool, pair = pos_ref[0], pos_ref[1]
    experts = [lax.rem(pool + s, n_pool) * n_pair + pair for s in range(n_pool)]
    for u in range(n_pair):
        hits, slots = picks(routes[u][...], experts)
        sel = jnp.concatenate([one_hot(hits, slots, s) for s in range(n_pool)], axis=0)
        rows = jnp.dot(sel.astype(BF16), tokens[u][...], preferred_element_type=F32).astype(BF16)
        for s in range(n_pool):
            outs[s][u * CAP : (u + 1) * CAP, :] = rows[s * CAP : (s + 1) * CAP]


def mixing_kernel(n_pool, n_pair, pos_ref, routes_ref, weights_ref, hi_ref, lo_ref):
    pool, pair = pos_ref[0], pos_ref[1]
    routes, weights = routes_ref[...], weights_ref[...]
    totals = jnp.sum(weights.astype(F32), axis=0, keepdims=True)
    experts = [
        lax.rem(pool + s, n_pool) * n_pair + lax.rem(pair - u + n_pair, n_pair)
        for u in range(n_pair)
        for s in range(n_pool)
    ]
    hits, slots = picks(routes, experts)
    for i, e in enumerate(experts):
        chosen = jnp.where(routes == e, weights, 0).astype(F32)
        share = jnp.sum(chosen, axis=0, keepdims=True) / totals
        mixing = one_hot(hits, slots, i) * share
        hi = mixing.astype(BF16)
        hi_ref[i * CAP : (i + 1) * CAP, :] = hi
        lo_ref[i * CAP : (i + 1) * CAP, :] = (mixing - hi.astype(F32)).astype(BF16)


def expert_kernel(n_tp, pos_ref, gate_ref, up_ref, down_ref, *refs):
    rows, outs = refs[:n_tp], refs[n_tp:]
    width = rows[0].shape[1]
    tp = pos_ref[2]
    gate = up = None
    for k in range(n_tp):
        at = pl.ds(pl.multiple_of(lax.rem(tp - k + n_tp, n_tp) * width, width), width)
        block = rows[k][...]
        g = jnp.dot(block, gate_ref[at, :], preferred_element_type=F32)
        u = jnp.dot(block, up_ref[at, :], preferred_element_type=F32)
        gate, up = (g, u) if gate is None else (gate + g, up + u)
    hidden = (gate / (1.0 + jnp.exp(-gate)) * up).astype(BF16)
    for k in range(n_tp):
        at = pl.ds(pl.multiple_of(lax.rem(tp + k, n_tp) * width, width), width)
        outs[k][...] = jnp.dot(hidden, down_ref[:, at], preferred_element_type=F32).astype(BF16)


def mix_kernel(n_pool, n_pair, hi_ref, lo_ref, *refs):
    home, away, out = refs[:n_pool], refs[n_pool:-1], refs[-1]
    rows = [r[:CAP, :] for r in home] + [r[...] for r in away]
    rows = jnp.concatenate(rows, axis=0)
    dims = (((0,), (0,)), ((), ()))
    total = lax.dot_general(hi_ref[...], rows, dims, preferred_element_type=F32)
    total += lax.dot_general(lo_ref[...], rows, dims, preferred_element_type=F32)
    out[...] = total.astype(BF16)


def turn(x, axis, shift):
    n = lax.axis_size(axis)
    return lax.ppermute(x, axis, [(i, (i + shift) % n) for i in range(n)])


def body(tokens, routes, gate_weights, w_gate, w_up, w_down):
    n_pool, n_tp, n_pair = (lax.axis_size(a) for a in ("pool", "tp", "pair"))
    streams, width = tokens.shape
    pos = jnp.stack([lax.axis_index(a) for a in ("pool", "pair", "tp")]).astype(jnp.int32)
    gate_mat, up_mat, down_mat = w_gate[0], w_up[0], w_down[0]
    routes_t = routes.T
    weights_t = gate_weights.T
    chunks = [[0], [1], [3], [2]] if n_pool == 4 else [list(range(n_pool))]

    all_tokens = [tokens] + [turn(tokens, "pair", -u) for u in range(1, n_pair)]
    all_routes = [routes_t] + [turn(routes_t, "pair", -u) for u in range(1, n_pair)]
    rows = n_pair * CAP
    leaving = pl.pallas_call(
        functools.partial(select_kernel, n_pool, n_pair, chunks),
        out_shape=[jax.ShapeDtypeStruct((rows, width), BF16)] * n_pool,
        in_specs=[SMEM] + [VMEM] * (2 * n_pair),
        out_specs=[VMEM] * n_pool,
        compiler_params=PARAMS,
        name="select",
    )(pos, *all_tokens, *all_routes)
    slots = n_pool * n_pair * CAP
    hi, lo = pl.pallas_call(
        functools.partial(mixing_kernel, n_pool, n_pair),
        out_shape=[jax.ShapeDtypeStruct((slots, streams), BF16)] * 2,
        in_specs=[SMEM, VMEM, VMEM],
        out_specs=[VMEM] * 2,
        compiler_params=PARAMS,
        name="mixing",
    )(pos, routes_t, weights_t)

    arrived = [turn(leaving[s], "pool", s) if s else leaving[0] for s in range(n_pool)]
    home = [None] * n_pool
    for chunk in chunks:
        block = arrived[chunk[0]] if len(chunk) == 1 else jnp.concatenate([arrived[s] for s in chunk])
        blocks = [block] + [turn(block, "tp", k) for k in range(1, n_tp)]
        parts = pl.pallas_call(
            functools.partial(expert_kernel, n_tp),
            out_shape=[jax.ShapeDtypeStruct((block.shape[0], width), BF16)] * n_tp,
            in_specs=[SMEM] + [VMEM] * (3 + n_tp),
            out_specs=[VMEM] * n_tp,
            compiler_params=PARAMS,
            name="expert",
        )(pos, gate_mat, up_mat, down_mat, *blocks)
        total = parts[0].astype(F32)
        for k in range(1, n_tp):
            total = total + turn(parts[k], "tp", k).astype(F32)
        total = total.astype(BF16)
        for i, s in enumerate(chunk):
            mine = total[i * rows : (i + 1) * rows]
            home[s] = turn(mine, "pool", -s) if s else mine
    away = [turn(home[s][u * CAP : (u + 1) * CAP], "pair", u) for u in range(1, n_pair) for s in range(n_pool)]
    return pl.pallas_call(
        functools.partial(mix_kernel, n_pool, n_pair),
        out_shape=jax.ShapeDtypeStruct((streams, width), BF16),
        in_specs=[VMEM] * (2 + n_pool * n_pair),
        out_specs=VMEM,
        compiler_params=PARAMS,
        name="mix",
    )(hi, lo, *home, *away)


def solution(mesh):
    in_specs = (
        P(("groups", "pool", "pair"), "tp"),
        P(("groups", "pool", "pair"), None),
        P(("groups", "pool", "pair"), None),
        P(("pool", "pair"), None, "tp"),
        P(("pool", "pair"), None, "tp"),
        P(("pool", "pair"), "tp", None),
    )
    out_specs = P(("groups", "pool", "pair"), "tp")
    return jax.shard_map(body, mesh=mesh, in_specs=in_specs, out_specs=out_specs, check_vma=False)
```

```python
import functools

import jax
import jax.numpy as jnp
from jax import lax
from jax.experimental import pallas as pl
from jax.experimental.pallas import tpu as pltpu
from jax.sharding import PartitionSpec as P

CAP = 16
VMEM = pl.BlockSpec(memory_space=pltpu.VMEM)
SMEM = pl.BlockSpec(memory_space=pltpu.SMEM)
HBM = pl.BlockSpec(memory_space=pltpu.HBM)
BF16, F32 = jnp.bfloat16, jnp.float32


def call(kernel, name, outs, in_specs, args, nbytes, flops=0, scratch=(), alias=None, vmem=24):
    return pl.pallas_call(
        kernel,
        out_shape=outs,
        in_specs=in_specs,
        out_specs=[VMEM] * len(outs),
        scratch_shapes=scratch,
        input_output_aliases=alias or {},
        compiler_params=pltpu.CompilerParams(vmem_limit_bytes=vmem * 2**20),
        cost_estimate=pl.CostEstimate(flops=flops, bytes_accessed=nbytes, transcendentals=0),
        name=name,
    )(*args)


def picks(routes_t, experts):
    hits = [
        jnp.max((routes_t == e).astype(F32), axis=0, keepdims=True) for e in experts
    ]
    hits = jnp.concatenate(hits, axis=0)
    streams = hits.shape[1]
    earlier = lax.broadcasted_iota(jnp.int32, (streams, streams), 0)
    later = lax.broadcasted_iota(jnp.int32, (streams, streams), 1)
    before = (earlier < later).astype(BF16)
    slots = jnp.dot(hits.astype(BF16), before, preferred_element_type=F32)
    return hits, slots


def one_hot(hits, slots, row):
    streams = hits.shape[1]
    slot = lax.broadcasted_iota(jnp.int32, (CAP, streams), 0).astype(F32)
    return jnp.where((slots[row : row + 1] == slot) & (hits[row : row + 1] > 0), 1.0, 0.0)


def select(pos_ref, routes, tokens, outs, n_pool, n_pair, u):
    pool, pair = pos_ref[0], pos_ref[1]
    experts = [lax.rem(pool + s, n_pool) * n_pair + pair for s in range(n_pool)]
    hits, slots = picks(routes[...], experts)
    sel = jnp.concatenate([one_hot(hits, slots, s) for s in range(n_pool)], axis=0)
    rows = jnp.dot(sel.astype(BF16), tokens[...], preferred_element_type=F32).astype(BF16)
    for s in range(n_pool):
        outs[s][u * CAP : (u + 1) * CAP, :] = rows[s * CAP : (s + 1) * CAP]


def select_own_kernel(n_pool, n_pair, pos_ref, routes, tokens, *refs):
    outs, held, sem = refs[:n_pool], refs[n_pool], refs[n_pool + 1]
    copy = pltpu.make_async_copy(tokens, held, sem)
    copy.start()
    copy.wait()
    select(pos_ref, routes, held, outs, n_pool, n_pair, 0)


def select_other_kernel(n_pool, n_pair, pos_ref, *refs):
    others = n_pair - 1
    routes, tokens = refs[:others], refs[others : 2 * others]
    outs = refs[2 * others + n_pool :]
    held = refs[2 * others : 2 * others + n_pool]
    for s in range(n_pool):
        outs[s][:CAP, :] = held[s][:CAP, :]
    for u in range(1, n_pair):
        select(pos_ref, routes[u - 1], tokens[u - 1], outs, n_pool, n_pair, u)


def mixing_kernel(n_pool, n_pair, pos_ref, after_ref, routes_ref, weights_ref, out_ref):
    pool, pair = pos_ref[0], pos_ref[1]
    routes, weights = routes_ref[...], weights_ref[...]
    totals = jnp.sum(weights.astype(F32), axis=0, keepdims=True)
    experts = [
        lax.rem(pool + s, n_pool) * n_pair + lax.rem(pair - u + n_pair, n_pair)
        for u in range(n_pair)
        for s in range(n_pool)
    ]
    hits, slots = picks(routes, experts)
    mixing = []
    for i, e in enumerate(experts):
        chosen = jnp.where(routes == e, weights, 0).astype(F32)
        share = jnp.sum(chosen, axis=0, keepdims=True) / totals
        mixing.append(one_hot(hits, slots, i) * share)
    mixing = jnp.concatenate(mixing, axis=0).T
    n = mixing.shape[1]
    hi = mixing.astype(BF16)
    out_ref[:, :n] = hi
    out_ref[:, n:] = (mixing - hi.astype(F32)).astype(BF16)


def load_kernel(after_ref, gate, up, gate_out, up_out, sems):
    pairs = ((gate, gate_out), (up, up_out))
    copies = [pltpu.make_async_copy(a, b, sems.at[i]) for i, (a, b) in enumerate(pairs)]
    for c in copies:
        c.start()
    for c in copies:
        c.wait()


def stacked(refs):
    return jnp.concatenate([r[...] for r in refs], axis=0)


def near_kernel(n_tp, pos_ref, gate_ref, up_ref, *refs):
    rows, gate_out, up_out = refs[:-2], refs[-2], refs[-1]
    width = rows[0].shape[1]
    at = pl.ds(pl.multiple_of(pos_ref[2] * width, width), width)
    block = stacked(rows)
    gate_out[...] = jnp.dot(block, gate_ref[at, :], preferred_element_type=F32)
    up_out[...] = jnp.dot(block, up_ref[at, :], preferred_element_type=F32)


def far_kernel(n_tp, n_chunks, pos_ref, gate_ref, up_ref, down_ref, gate_in, up_in, *refs):
    far = n_tp - 1
    rows = [refs[k * n_chunks : (k + 1) * n_chunks] for k in range(far)]
    hidden_ref, outs = refs[far * n_chunks], refs[far * n_chunks + 1 :]
    width = down_ref.shape[1] // n_tp
    tp = pos_ref[2]
    gate, up = gate_in[...], up_in[...]
    for k in range(1, n_tp):
        at = pl.ds(pl.multiple_of(lax.rem(tp - k + n_tp, n_tp) * width, width), width)
        block = stacked(rows[k - 1])
        gate += jnp.dot(block, gate_ref[at, :], preferred_element_type=F32)
        up += jnp.dot(block, up_ref[at, :], preferred_element_type=F32)
    hidden = (gate / (1.0 + jnp.exp(-gate)) * up).astype(BF16)
    hidden_ref[...] = hidden
    for k in range(1, n_tp):
        at = pl.ds(pl.multiple_of(lax.rem(tp + k, n_tp) * width, width), width)
        part = jnp.dot(hidden, down_ref[:, at], preferred_element_type=F32).astype(BF16)
        put(outs[(k - 1) * n_chunks : k * n_chunks], part)


def put(outs, part):
    at = 0
    for o in outs:
        o[...] = part[at : at + o.shape[0]]
        at += o.shape[0]


def keep_kernel(n_tp, pos_ref, down_ref, hidden_ref, *outs):
    width = outs[0].shape[1]
    at = pl.ds(pl.multiple_of(pos_ref[2] * width, width), width)
    put(outs, jnp.dot(hidden_ref[...], down_ref[:, at], preferred_element_type=F32).astype(BF16))


def mix_kernel(n_pool, n_pair, layout, mixing_ref, *refs):
    parts, out = refs[:-1], refs[-1]
    at, rows = 0, []
    for n, first in layout:
        total = parts[at][first : first + CAP, :].astype(F32)
        for r in parts[at + 1 : at + n]:
            total += r[first : first + CAP, :].astype(F32)
        rows.append(total.astype(BF16))
        at += n
    rows = jnp.concatenate(rows + rows, axis=0)
    out[...] = jnp.dot(mixing_ref[...], rows, preferred_element_type=F32).astype(BF16)


def turn(x, axis, shift):
    n = lax.axis_size(axis)
    return lax.ppermute(x, axis, [(i, (i + shift) % n) for i in range(n)])


def cross(x, shift, k):
    n, m = lax.axis_size("pool"), lax.axis_size("tp")
    pairs = [(i * m + j, (i + shift) % n * m + (j + k) % m) for i in range(n) for j in range(m)]
    return lax.ppermute(x, ("pool", "tp"), pairs)


def add(parts):
    total = parts[0].astype(F32)
    for p in parts[1:]:
        total += p.astype(F32)
    return total.astype(BF16)


def body(tokens, routes, gate_weights, w_gate, w_up, w_down):
    n_pool, n_tp, n_pair = (lax.axis_size(a) for a in ("pool", "tp", "pair"))
    streams, width = tokens.shape
    hidden_units = w_gate.shape[2]
    pos = jnp.stack([lax.axis_index(a) for a in ("pool", "pair", "tp")]).astype(jnp.int32)
    routes_t, weights_t = routes.T, gate_weights.T
    rows = n_pair * CAP
    small = n_pool <= 4 and n_tp == 2
    direct = [1] if small else []

    def shape(r, c, t=BF16):
        return jax.ShapeDtypeStruct((r, c), t)

    far_tokens = [turn(tokens, "pair", -u) for u in range(1, n_pair)]
    far_routes = [turn(routes_t, "pair", -u) for u in range(1, n_pair)]
    leaving = call(
        functools.partial(select_own_kernel, n_pool, n_pair),
        "select_own",
        [shape(rows, width)] * n_pool,
        [SMEM, VMEM, HBM],
        (pos, routes_t, tokens),
        2 * 2 * streams * width,
        scratch=[pltpu.VMEM((streams, width), BF16), pltpu.SemaphoreType.DMA],
    )
    leaving = call(
        functools.partial(select_other_kernel, n_pool, n_pair),
        "select_other",
        [shape(rows, width)] * n_pool,
        [SMEM] + [VMEM] * (2 * (n_pair - 1) + n_pool),
        (pos, *far_routes, *far_tokens, *leaving),
        2 * 2 * streams * width,
        alias={1 + 2 * (n_pair - 1) + s: s for s in range(n_pool)},
    )
    gate_mat, up_mat = call(
        load_kernel,
        "load",
        [jax.ShapeDtypeStruct(w.shape[1:], BF16) for w in (w_gate, w_up)],
        [VMEM] + [HBM] * 2,
        (leaving[0], w_gate[0], w_up[0]),
        2 * 2 * (w_gate.size + w_up.size),
        scratch=[pltpu.SemaphoreType.DMA((2,))],
        vmem=44,
    )
    down_mat = w_down[0]
    slots = n_pool * rows
    (mixing,) = call(
        functools.partial(mixing_kernel, n_pool, n_pair),
        "mixing",
        [shape(streams, 2 * slots)],
        [SMEM, VMEM, VMEM, VMEM],
        (pos, leaving[0], routes_t, weights_t),
        4 * 10 * streams * slots,
    )

    near = [turn(leaving[s], "pool", s) if s else leaving[0] for s in range(n_pool)]
    first = 1 if n_pool > 1 else 0
    near[first], gate_mat, up_mat, mixing = lax.optimization_barrier((near[first], gate_mat, up_mat, mixing))
    far = [[turn(b, "tp", k) for b in near] for k in range(1, n_tp)]
    gate, up = call(
        functools.partial(near_kernel, n_tp),
        "near",
        [shape(slots, hidden_units, F32)] * 2,
        [SMEM] + [VMEM] * (2 + n_pool),
        (pos, gate_mat, up_mat, *near),
        4 * width * hidden_units,
        4 * slots * width * hidden_units,
    )
    hidden, *sent = call(
        functools.partial(far_kernel, n_tp, n_pool),
        "far",
        [shape(slots, hidden_units)] + [shape(rows, width)] * (n_pool * (n_tp - 1)),
        [SMEM] + [VMEM] * (5 + n_pool * (n_tp - 1)),
        (pos, gate_mat, up_mat, down_mat, gate, up, *sum(far, [])),
        8 * width * hidden_units,
        6 * slots * width * hidden_units,
    )
    sent = [sent[k * n_pool : (k + 1) * n_pool] for k in range(n_tp - 1)]
    kept = call(
        functools.partial(keep_kernel, n_tp),
        "keep",
        [shape(rows, width)] * n_pool,
        [SMEM] + [VMEM] * 2,
        (pos, down_mat, hidden),
        2 * width * hidden_units,
        2 * slots * width * hidden_units,
    )

    home = []
    for s in range(n_pool):
        if s in direct:
            home.append([cross(kept[s], -s, 0)] + [cross(sent[k - 1][s], -s, k) for k in range(1, n_tp)])
        else:
            total = add([kept[s]] + [turn(sent[k - 1][s], "tp", k) for k in range(1, n_tp)])
            home.append([turn(total, "pool", -s) if s else total])
    layout, parts = [], []
    for s in range(n_pool):
        layout.append((len(home[s]), 0))
        parts += home[s]
    for u in range(1, n_pair):
        for s in range(n_pool):
            part = add([h[u * CAP : (u + 1) * CAP] for h in home[s]])
            layout.append((1, 0))
            parts.append(turn(part, "pair", u))
    (out,) = call(
        functools.partial(mix_kernel, n_pool, n_pair, layout),
        "mix",
        [shape(streams, width)],
        [VMEM] * (1 + len(parts)),
        (mixing, *parts),
        2 * 3 * streams * width,
    )
    return out


def solution(mesh):
    in_specs = (
        P(("groups", "pool", "pair"), "tp"),
        P(("groups", "pool", "pair"), None),
        P(("groups", "pool", "pair"), None),
        P(("pool", "pair"), None, "tp"),
        P(("pool", "pair"), None, "tp"),
        P(("pool", "pair"), "tp", None),
    )
    out_specs = P(("groups", "pool", "pair"), "tp")
    return jax.shard_map(body, mesh=mesh, in_specs=in_specs, out_specs=out_specs, check_vma=False)
```

```python
import functools

import jax
import jax.numpy as jnp
from jax import lax
from jax.experimental import pallas as pl
from jax.experimental.pallas import tpu as pltpu
from jax.sharding import PartitionSpec as P

CAP = 16
VMEM = pl.BlockSpec(memory_space=pltpu.VMEM)
SMEM = pl.BlockSpec(memory_space=pltpu.SMEM)
HBM = pl.BlockSpec(memory_space=pltpu.HBM)
BF16, F32 = jnp.bfloat16, jnp.float32


def call(kernel, name, outs, in_specs, args, nbytes, flops=0, scratch=(), alias=None, vmem=24):
    return pl.pallas_call(
        kernel,
        out_shape=outs,
        in_specs=in_specs,
        out_specs=[VMEM] * len(outs),
        scratch_shapes=scratch,
        input_output_aliases=alias or {},
        compiler_params=pltpu.CompilerParams(vmem_limit_bytes=vmem * 2**20),
        cost_estimate=pl.CostEstimate(flops=flops, bytes_accessed=nbytes, transcendentals=0),
        name=name,
    )(*args)


def picks(routes_t, experts):
    hits = [
        jnp.max((routes_t == e).astype(F32), axis=0, keepdims=True) for e in experts
    ]
    hits = jnp.concatenate(hits, axis=0)
    streams = hits.shape[1]
    earlier = lax.broadcasted_iota(jnp.int32, (streams, streams), 0)
    later = lax.broadcasted_iota(jnp.int32, (streams, streams), 1)
    before = (earlier < later).astype(BF16)
    slots = jnp.dot(hits.astype(BF16), before, preferred_element_type=F32)
    return hits, slots


def one_hot(hits, slots, row):
    streams = hits.shape[1]
    slot = lax.broadcasted_iota(jnp.int32, (CAP, streams), 0).astype(F32)
    return jnp.where((slots[row : row + 1] == slot) & (hits[row : row + 1] > 0), 1.0, 0.0)


def select(pos_ref, routes, tokens, outs, n_pool, n_pair, u):
    pool, pair = pos_ref[0], pos_ref[1]
    experts = [lax.rem(pool + s, n_pool) * n_pair + pair for s in range(n_pool)]
    hits, slots = picks(routes[...], experts)
    sel = jnp.concatenate([one_hot(hits, slots, s) for s in range(n_pool)], axis=0)
    rows = jnp.dot(sel.astype(BF16), tokens[...], preferred_element_type=F32).astype(BF16)
    for s in range(n_pool):
        outs[s][u * CAP : (u + 1) * CAP, :] = rows[s * CAP : (s + 1) * CAP]


def select_own_kernel(n_pool, n_pair, pos_ref, routes, tokens, *refs):
    outs, held, sem = refs[:n_pool], refs[n_pool], refs[n_pool + 1]
    copy = pltpu.make_async_copy(tokens, held, sem)
    copy.start()
    copy.wait()
    select(pos_ref, routes, held, outs, n_pool, n_pair, 0)


def select_other_kernel(n_pool, n_pair, pos_ref, *refs):
    others = n_pair - 1
    routes, tokens = refs[:others], refs[others : 2 * others]
    outs = refs[2 * others + n_pool :]
    held = refs[2 * others : 2 * others + n_pool]
    for s in range(n_pool):
        outs[s][:CAP, :] = held[s][:CAP, :]
    for u in range(1, n_pair):
        select(pos_ref, routes[u - 1], tokens[u - 1], outs, n_pool, n_pair, u)


def mixing_kernel(n_pool, n_pair, pos_ref, after_ref, routes_ref, weights_ref, out_ref):
    pool, pair = pos_ref[0], pos_ref[1]
    routes, weights = routes_ref[...], weights_ref[...]
    totals = jnp.sum(weights.astype(F32), axis=0, keepdims=True)
    experts = [
        lax.rem(pool + s, n_pool) * n_pair + lax.rem(pair - u + n_pair, n_pair)
        for u in range(n_pair)
        for s in range(n_pool)
    ]
    hits, slots = picks(routes, experts)
    mixing = []
    for i, e in enumerate(experts):
        chosen = jnp.where(routes == e, weights, 0).astype(F32)
        share = jnp.sum(chosen, axis=0, keepdims=True) / totals
        mixing.append(one_hot(hits, slots, i) * share)
    mixing = jnp.concatenate(mixing, axis=0).T
    n = mixing.shape[1]
    hi = mixing.astype(BF16)
    out_ref[:, :n] = hi
    out_ref[:, n:] = (mixing - hi.astype(F32)).astype(BF16)


def stacked(refs):
    return jnp.concatenate([r[...] for r in refs], axis=0)


def near_kernel(n_tp, tiles, pos_ref, gate_ref, up_ref, *refs):
    rows = refs[:-7]
    gate_out, up_out, gate_far, up_far, gate_near, up_near, sems = refs[-7:]
    width = rows[0].shape[1]
    tp = pos_ref[2]
    depth = width // tiles
    pairs = ((gate_ref, gate_near, gate_far), (up_ref, up_near, up_far))
    near, far = [], []
    for i in range(tiles):
        at = pl.ds(pl.multiple_of(tp * width + i * depth, depth), depth)
        for j, (ref, held, _) in enumerate(pairs):
            near.append(pltpu.make_async_copy(ref.at[at, :], held.at[pl.ds(i * depth, depth), :], sems.at[i * 2 + j]))
    for k in range(1, n_tp):
        for i in range(2):
            half = width // 2
            at = pl.ds(pl.multiple_of(lax.rem(tp - k + n_tp, n_tp) * width + i * half, half), half)
            to = pl.ds((k - 1) * width + i * half, half)
            for j, (ref, _, out) in enumerate(pairs):
                sem = sems.at[2 * tiles + ((k - 1) * 2 + i) * 2 + j]
                far.append(pltpu.make_async_copy(ref.at[at, :], out.at[to, :], sem))
    for c in near + far:
        c.start()
    block = stacked(rows)
    gate = up = None
    for i in range(tiles):
        cut = block[:, i * depth : (i + 1) * depth]
        near[2 * i].wait()
        g = jnp.dot(cut, gate_near[i * depth : (i + 1) * depth, :], preferred_element_type=F32)
        near[2 * i + 1].wait()
        u = jnp.dot(cut, up_near[i * depth : (i + 1) * depth, :], preferred_element_type=F32)
        gate, up = (g, u) if gate is None else (gate + g, up + u)
    gate_out[...] = gate
    up_out[...] = up
    for c in far:
        c.wait()


def far_kernel(n_tp, n_chunks, pos_ref, gate_ref, up_ref, down_ref, gate_in, up_in, *refs):
    far = n_tp - 1
    rows = [refs[k * n_chunks : (k + 1) * n_chunks] for k in range(far)]
    hidden_ref, outs = refs[far * n_chunks], refs[far * n_chunks + 1 :]
    width = down_ref.shape[1] // n_tp
    tp = pos_ref[2]
    gate, up = gate_in[...], up_in[...]
    for k in range(1, n_tp):
        at = pl.ds((k - 1) * width, width)
        block = stacked(rows[k - 1])
        gate += jnp.dot(block, gate_ref[at, :], preferred_element_type=F32)
        up += jnp.dot(block, up_ref[at, :], preferred_element_type=F32)
    hidden = (gate / (1.0 + jnp.exp(-gate)) * up).astype(BF16)
    hidden_ref[...] = hidden
    for k in range(1, n_tp):
        at = pl.ds(pl.multiple_of(lax.rem(tp + k, n_tp) * width, width), width)
        part = jnp.dot(hidden, down_ref[:, at], preferred_element_type=F32).astype(BF16)
        put(outs[(k - 1) * n_chunks : k * n_chunks], part)


def put(outs, part):
    at = 0
    for o in outs:
        o[...] = part[at : at + o.shape[0]]
        at += o.shape[0]


def keep_kernel(n_tp, pos_ref, down_ref, hidden_ref, *outs):
    width = outs[0].shape[1]
    at = pl.ds(pl.multiple_of(pos_ref[2] * width, width), width)
    put(outs, jnp.dot(hidden_ref[...], down_ref[:, at], preferred_element_type=F32).astype(BF16))


def mix_kernel(n_pool, n_pair, layout, mixing_ref, *refs):
    parts, out = refs[:-1], refs[-1]
    at, rows = 0, []
    for n, first in layout:
        total = parts[at][first : first + CAP, :].astype(F32)
        for r in parts[at + 1 : at + n]:
            total += r[first : first + CAP, :].astype(F32)
        rows.append(total.astype(BF16))
        at += n
    rows = jnp.concatenate(rows + rows, axis=0)
    out[...] = jnp.dot(mixing_ref[...], rows, preferred_element_type=F32).astype(BF16)


def turn(x, axis, shift):
    n = lax.axis_size(axis)
    return lax.ppermute(x, axis, [(i, (i + shift) % n) for i in range(n)])


def cross(x, shift, k):
    n, m = lax.axis_size("pool"), lax.axis_size("tp")
    pairs = [(i * m + j, (i + shift) % n * m + (j + k) % m) for i in range(n) for j in range(m)]
    return lax.ppermute(x, ("pool", "tp"), pairs)


def add(parts):
    total = parts[0].astype(F32)
    for p in parts[1:]:
        total += p.astype(F32)
    return total.astype(BF16)


def body(tokens, routes, gate_weights, w_gate, w_up, w_down):
    n_pool, n_tp, n_pair = (lax.axis_size(a) for a in ("pool", "tp", "pair"))
    streams, width = tokens.shape
    hidden_units = w_gate.shape[2]
    pos = jnp.stack([lax.axis_index(a) for a in ("pool", "pair", "tp")]).astype(jnp.int32)
    routes_t, weights_t = routes.T, gate_weights.T
    rows = n_pair * CAP
    small = n_pool == 4 and n_tp == 2
    direct = [1] if small else []

    def shape(r, c, t=BF16):
        return jax.ShapeDtypeStruct((r, c), t)

    far_tokens = [turn(tokens, "pair", -u) for u in range(1, n_pair)]
    far_routes = [turn(routes_t, "pair", -u) for u in range(1, n_pair)]
    leaving = call(
        functools.partial(select_own_kernel, n_pool, n_pair),
        "select_own",
        [shape(rows, width)] * n_pool,
        [SMEM, VMEM, HBM],
        (pos, routes_t, tokens),
        2 * 2 * streams * width,
        scratch=[pltpu.VMEM((streams, width), BF16), pltpu.SemaphoreType.DMA],
    )
    leaving = call(
        functools.partial(select_other_kernel, n_pool, n_pair),
        "select_other",
        [shape(rows, width)] * n_pool,
        [SMEM] + [VMEM] * (2 * (n_pair - 1) + n_pool),
        (pos, *far_routes, *far_tokens, *leaving),
        2 * 2 * streams * width,
        alias={1 + 2 * (n_pair - 1) + s: s for s in range(n_pool)},
    )
    gate_mat, up_mat, down_mat = w_gate[0], w_up[0], w_down[0]
    slots = n_pool * rows
    (mixing,) = call(
        functools.partial(mixing_kernel, n_pool, n_pair),
        "mixing",
        [shape(streams, 2 * slots)],
        [SMEM, VMEM, VMEM, VMEM],
        (pos, leaving[0], routes_t, weights_t),
        4 * 10 * streams * slots,
    )

    near = [turn(leaving[s], "pool", s) if s else leaving[0] for s in range(n_pool)]
    first = 1 if n_pool > 1 else 0
    near[first], mixing = lax.optimization_barrier((near[first], mixing))
    far = [[turn(b, "tp", k) for b in near] for k in range(1, n_tp)]
    tiles = 4 if width % 1024 == 0 else 1
    rest = (n_tp - 1) * width
    gate, up, gate_far, up_far = call(
        functools.partial(near_kernel, n_tp, tiles),
        "near",
        [shape(slots, hidden_units, F32)] * 2 + [shape(rest, hidden_units)] * 2,
        [SMEM] + [HBM] * 2 + [VMEM] * n_pool,
        (pos, gate_mat, up_mat, *near),
        2 * 2 * (w_gate.size + w_up.size),
        4 * slots * width * hidden_units,
        scratch=[pltpu.VMEM((width, hidden_units), BF16)] * 2
        + [pltpu.SemaphoreType.DMA((2 * tiles + 4 * (n_tp - 1),))],
        vmem=48,
    )
    hidden, *sent = call(
        functools.partial(far_kernel, n_tp, n_pool),
        "far",
        [shape(slots, hidden_units)] + [shape(rows, width)] * (n_pool * (n_tp - 1)),
        [SMEM] + [VMEM] * (5 + n_pool * (n_tp - 1)),
        (pos, gate_far, up_far, down_mat, gate, up, *sum(far, [])),
        8 * width * hidden_units,
        6 * slots * width * hidden_units,
    )
    sent = [sent[k * n_pool : (k + 1) * n_pool] for k in range(n_tp - 1)]
    kept = call(
        functools.partial(keep_kernel, n_tp),
        "keep",
        [shape(rows, width)] * n_pool,
        [SMEM] + [VMEM] * 2,
        (pos, down_mat, hidden),
        2 * width * hidden_units,
        2 * slots * width * hidden_units,
    )

    home = [None] * n_pool
    for s in [2, 1, 3, 0] if small else range(n_pool):
        if s in direct:
            home[s] = [cross(kept[s], -s, 0)] + [cross(sent[k - 1][s], -s, k) for k in range(1, n_tp)]
        else:
            come = [turn(sent[k - 1][s], "tp", k) for k in range(1, n_tp)]
            total = add([kept[s]] + come)
            if small and s == 3:
                total, sent[0][0] = lax.optimization_barrier((total, sent[0][0]))
            home[s] = [turn(total, "pool", -s) if s else total]
    if small:
        home[1], home[0] = lax.optimization_barrier((home[1], home[0]))
    layout, parts = [], []
    for s in range(n_pool):
        layout.append((len(home[s]), 0))
        parts += home[s]
    for u in range(1, n_pair):
        for s in range(n_pool):
            part = add([h[u * CAP : (u + 1) * CAP] for h in home[s]])
            layout.append((1, 0))
            parts.append(turn(part, "pair", u))
    (out,) = call(
        functools.partial(mix_kernel, n_pool, n_pair, layout),
        "mix",
        [shape(streams, width)],
        [VMEM] * (1 + len(parts)),
        (mixing, *parts),
        2 * 3 * streams * width,
    )
    return out


def solution(mesh):
    in_specs = (
        P(("groups", "pool", "pair"), "tp"),
        P(("groups", "pool", "pair"), None),
        P(("groups", "pool", "pair"), None),
        P(("pool", "pair"), None, "tp"),
        P(("pool", "pair"), None, "tp"),
        P(("pool", "pair"), "tp", None),
    )
    out_specs = P(("groups", "pool", "pair"), "tp")
    return jax.shard_map(body, mesh=mesh, in_specs=in_specs, out_specs=out_specs, check_vma=False)
```

```python
import functools

import jax
import jax.numpy as jnp
from jax import lax
from jax.experimental import pallas as pl
from jax.experimental.pallas import tpu as pltpu
from jax.sharding import PartitionSpec as P

CAP = 16
VMEM = pl.BlockSpec(memory_space=pltpu.VMEM)
SMEM = pl.BlockSpec(memory_space=pltpu.SMEM)
HBM = pl.BlockSpec(memory_space=pltpu.HBM)
BF16, F32 = jnp.bfloat16, jnp.float32


def call(kernel, name, outs, in_specs, args, nbytes, flops=0, scratch=(), alias=None, vmem=24):
    return pl.pallas_call(
        kernel,
        out_shape=outs,
        in_specs=in_specs,
        out_specs=[VMEM] * len(outs),
        scratch_shapes=scratch,
        input_output_aliases=alias or {},
        compiler_params=pltpu.CompilerParams(vmem_limit_bytes=vmem * 2**20),
        cost_estimate=pl.CostEstimate(flops=flops, bytes_accessed=nbytes, transcendentals=0),
        name=name,
    )(*args)


def picks(routes_t, experts):
    hits = [
        jnp.max((routes_t == e).astype(F32), axis=0, keepdims=True) for e in experts
    ]
    hits = jnp.concatenate(hits, axis=0)
    streams = hits.shape[1]
    earlier = lax.broadcasted_iota(jnp.int32, (streams, streams), 0)
    later = lax.broadcasted_iota(jnp.int32, (streams, streams), 1)
    before = (earlier < later).astype(BF16)
    slots = jnp.dot(hits.astype(BF16), before, preferred_element_type=F32)
    return hits, slots


def one_hot(hits, slots, row):
    streams = hits.shape[1]
    slot = lax.broadcasted_iota(jnp.int32, (CAP, streams), 0).astype(F32)
    return jnp.where((slots[row : row + 1] == slot) & (hits[row : row + 1] > 0), 1.0, 0.0)


def select(pos_ref, routes, tokens, outs, n_pool, n_pair, u, copy=None):
    pool, pair = pos_ref[0], pos_ref[1]
    experts = [lax.rem(pool + s, n_pool) * n_pair + pair for s in range(n_pool)]
    hits, slots = picks(routes[...], experts)
    sel = jnp.concatenate([one_hot(hits, slots, s) for s in range(n_pool)], axis=0)
    if copy is not None:
        copy.wait()
    rows = jnp.dot(sel.astype(BF16), tokens[...], preferred_element_type=F32).astype(BF16)
    for s in range(n_pool):
        outs[s][u * CAP : (u + 1) * CAP, :] = rows[s * CAP : (s + 1) * CAP]


def select_own_kernel(n_pool, n_pair, pos_ref, routes, tokens, *refs):
    outs, held, held_routes, sems = refs[:n_pool], refs[n_pool], refs[n_pool + 1], refs[n_pool + 2]
    first = pltpu.make_async_copy(routes, held_routes, sems.at[0])
    second = pltpu.make_async_copy(tokens, held, sems.at[1])
    first.start()
    second.start()
    first.wait()
    select(pos_ref, held_routes, held, outs, n_pool, n_pair, 0, second)


def select_other_kernel(n_pool, n_pair, pos_ref, *refs):
    others = n_pair - 1
    routes, tokens = refs[:others], refs[others : 2 * others]
    outs = refs[2 * others + n_pool :]
    held = refs[2 * others : 2 * others + n_pool]
    for s in range(n_pool):
        outs[s][:CAP, :] = held[s][:CAP, :]
    for u in range(1, n_pair):
        select(pos_ref, routes[u - 1], tokens[u - 1], outs, n_pool, n_pair, u)


def mixing_kernel(n_pool, n_pair, pos_ref, after_ref, routes_ref, weights_ref, out_ref):
    pool, pair = pos_ref[0], pos_ref[1]
    routes, weights = routes_ref[...], weights_ref[...]
    totals = jnp.sum(weights.astype(F32), axis=0, keepdims=True)
    experts = [
        lax.rem(pool + s, n_pool) * n_pair + lax.rem(pair - u + n_pair, n_pair)
        for u in range(n_pair)
        for s in range(n_pool)
    ]
    hits, slots = picks(routes, experts)
    mixing = []
    for i, e in enumerate(experts):
        chosen = jnp.where(routes == e, weights, 0).astype(F32)
        share = jnp.sum(chosen, axis=0, keepdims=True) / totals
        mixing.append(one_hot(hits, slots, i) * share)
    mixing = jnp.concatenate(mixing, axis=0).T
    n = mixing.shape[1]
    hi = mixing.astype(BF16)
    out_ref[:, :n] = hi
    out_ref[:, n:] = (mixing - hi.astype(F32)).astype(BF16)


def stacked(refs):
    return jnp.concatenate([r[...] for r in refs], axis=0)


def near_kernel(n_tp, tiles, pos_ref, gate_ref, up_ref, *refs):
    rows = refs[:-7]
    gate_out, up_out, gate_far, up_far, gate_near, up_near, sems = refs[-7:]
    width = rows[0].shape[1]
    tp = pos_ref[2]
    depth = width // tiles
    pairs = ((gate_ref, gate_near, gate_far), (up_ref, up_near, up_far))
    near, far = [], []
    for i in range(tiles):
        at = pl.ds(pl.multiple_of(tp * width + i * depth, depth), depth)
        for j, (ref, held, _) in enumerate(pairs):
            near.append(pltpu.make_async_copy(ref.at[at, :], held.at[pl.ds(i * depth, depth), :], sems.at[i * 2 + j]))
    for k in range(1, n_tp):
        for i in range(2):
            half = width // 2
            at = pl.ds(pl.multiple_of(lax.rem(tp - k + n_tp, n_tp) * width + i * half, half), half)
            to = pl.ds((k - 1) * width + i * half, half)
            for j, (ref, _, out) in enumerate(pairs):
                sem = sems.at[2 * tiles + ((k - 1) * 2 + i) * 2 + j]
                far.append(pltpu.make_async_copy(ref.at[at, :], out.at[to, :], sem))
    for c in near + far:
        c.start()
    block = stacked(rows)
    gate = up = None
    for i in range(tiles):
        cut = block[:, i * depth : (i + 1) * depth]
        near[2 * i].wait()
        g = jnp.dot(cut, gate_near[i * depth : (i + 1) * depth, :], preferred_element_type=F32)
        near[2 * i + 1].wait()
        u = jnp.dot(cut, up_near[i * depth : (i + 1) * depth, :], preferred_element_type=F32)
        gate, up = (g, u) if gate is None else (gate + g, up + u)
    gate_out[...] = gate
    up_out[...] = up
    for c in far:
        c.wait()


def far_kernel(n_tp, n_chunks, pos_ref, gate_ref, up_ref, down_ref, gate_in, up_in, *refs):
    far = n_tp - 1
    rows = [refs[k * n_chunks : (k + 1) * n_chunks] for k in range(far)]
    hidden_ref, outs = refs[far * n_chunks], refs[far * n_chunks + 1 :]
    width = down_ref.shape[1] // n_tp
    tp = pos_ref[2]
    gate, up = gate_in[...], up_in[...]
    for k in range(1, n_tp):
        at = pl.ds((k - 1) * width, width)
        block = stacked(rows[k - 1])
        gate += jnp.dot(block, gate_ref[at, :], preferred_element_type=F32)
        up += jnp.dot(block, up_ref[at, :], preferred_element_type=F32)
    hidden = (gate / (1.0 + jnp.exp(-gate)) * up).astype(BF16)
    hidden_ref[...] = hidden
    for k in range(1, n_tp):
        at = pl.ds(pl.multiple_of(lax.rem(tp + k, n_tp) * width, width), width)
        part = jnp.dot(hidden, down_ref[:, at], preferred_element_type=F32).astype(BF16)
        put(outs[(k - 1) * n_chunks : k * n_chunks], part)


def put(outs, part):
    at = 0
    for o in outs:
        o[...] = part[at : at + o.shape[0]]
        at += o.shape[0]


def keep_kernel(n_tp, pos_ref, down_ref, hidden_ref, *outs):
    width = outs[0].shape[1]
    at = pl.ds(pl.multiple_of(pos_ref[2] * width, width), width)
    put(outs, jnp.dot(hidden_ref[...], down_ref[:, at], preferred_element_type=F32).astype(BF16))


def mix_kernel(n_pool, n_pair, layout, mixing_ref, *refs):
    parts, out = refs[:-1], refs[-1]
    at, rows = 0, []
    for n, first in layout:
        total = parts[at][first : first + CAP, :].astype(F32)
        for r in parts[at + 1 : at + n]:
            total += r[first : first + CAP, :].astype(F32)
        rows.append(total.astype(BF16))
        at += n
    rows = jnp.concatenate(rows + rows, axis=0)
    out[...] = jnp.dot(mixing_ref[...], rows, preferred_element_type=F32).astype(BF16)


def turn(x, axis, shift):
    n = lax.axis_size(axis)
    return lax.ppermute(x, axis, [(i, (i + shift) % n) for i in range(n)])


def cross(x, shift, k):
    n, m = lax.axis_size("pool"), lax.axis_size("tp")
    pairs = [(i * m + j, (i + shift) % n * m + (j + k) % m) for i in range(n) for j in range(m)]
    return lax.ppermute(x, ("pool", "tp"), pairs)


def add(parts):
    total = parts[0].astype(F32)
    for p in parts[1:]:
        total += p.astype(F32)
    return total.astype(BF16)


def body(tokens, routes, gate_weights, w_gate, w_up, w_down):
    n_pool, n_tp, n_pair = (lax.axis_size(a) for a in ("pool", "tp", "pair"))
    streams, width = tokens.shape
    hidden_units = w_gate.shape[2]
    pos = jnp.stack([lax.axis_index(a) for a in ("pool", "pair", "tp")]).astype(jnp.int32)
    routes_t, weights_t = routes.T, gate_weights.T
    rows = n_pair * CAP
    small = n_pool == 4 and n_tp == 2
    direct = []

    def shape(r, c, t=BF16):
        return jax.ShapeDtypeStruct((r, c), t)

    far_tokens = [turn(tokens, "pair", -u) for u in range(1, n_pair)]
    far_routes = [turn(routes_t, "pair", -u) for u in range(1, n_pair)]
    leaving = call(
        functools.partial(select_own_kernel, n_pool, n_pair),
        "select_own",
        [shape(rows, width)] * n_pool,
        [SMEM, HBM, HBM],
        (pos, pltpu.with_memory_space_constraint(routes_t, pltpu.HBM), pltpu.with_memory_space_constraint(tokens, pltpu.HBM)),
        2 * 2 * streams * width,
        scratch=[
            pltpu.VMEM((streams, width), BF16),
            pltpu.VMEM(routes_t.shape, routes.dtype),
            pltpu.SemaphoreType.DMA((2,)),
        ],
    )
    leaving = call(
        functools.partial(select_other_kernel, n_pool, n_pair),
        "select_other",
        [shape(rows, width)] * n_pool,
        [SMEM] + [VMEM] * (2 * (n_pair - 1) + n_pool),
        (pos, *far_routes, *far_tokens, *leaving),
        2 * 2 * streams * width,
        alias={1 + 2 * (n_pair - 1) + s: s for s in range(n_pool)},
    )
    gate_mat, up_mat, down_mat = w_gate[0], w_up[0], w_down[0]
    slots = n_pool * rows
    (mixing,) = call(
        functools.partial(mixing_kernel, n_pool, n_pair),
        "mixing",
        [shape(streams, 2 * slots)],
        [SMEM, VMEM, VMEM, VMEM],
        (pos, leaving[0], routes_t, weights_t),
        4 * 10 * streams * slots,
    )

    near = [leaving[0]] * n_pool
    for s in [3, 2, 1] if small else range(1, n_pool):
        near[s] = turn(leaving[s], "pool", s)
    first = 3 if small else 0
    near[first], mixing = lax.optimization_barrier((near[first], mixing))
    far = [[turn(b, "tp", k) for b in near] for k in range(1, n_tp)]
    tiles = 4 if width % 1024 == 0 else 1
    rest = (n_tp - 1) * width
    gate, up, gate_far, up_far = call(
        functools.partial(near_kernel, n_tp, tiles),
        "near",
        [shape(slots, hidden_units, F32)] * 2 + [shape(rest, hidden_units)] * 2,
        [SMEM] + [HBM] * 2 + [VMEM] * n_pool,
        (pos, gate_mat, up_mat, *near),
        2 * 2 * (w_gate.size + w_up.size),
        4 * slots * width * hidden_units,
        scratch=[pltpu.VMEM((width, hidden_units), BF16)] * 2
        + [pltpu.SemaphoreType.DMA((2 * tiles + 4 * (n_tp - 1),))],
        vmem=48,
    )
    hidden, *sent = call(
        functools.partial(far_kernel, n_tp, n_pool),
        "far",
        [shape(slots, hidden_units)] + [shape(rows, width)] * (n_pool * (n_tp - 1)),
        [SMEM] + [VMEM] * (5 + n_pool * (n_tp - 1)),
        (pos, gate_far, up_far, down_mat, gate, up, *sum(far, [])),
        8 * width * hidden_units,
        6 * slots * width * hidden_units,
    )
    sent = [sent[k * n_pool : (k + 1) * n_pool] for k in range(n_tp - 1)]
    kept = call(
        functools.partial(keep_kernel, n_tp),
        "keep",
        [shape(rows, width)] * n_pool,
        [SMEM] + [VMEM] * 2,
        (pos, down_mat, hidden),
        2 * width * hidden_units,
        2 * slots * width * hidden_units,
    )

    home = [None] * n_pool
    totals = [None] * n_pool
    for s in [2, 3, 1, 0] if small else range(n_pool):
        if s in direct:
            home[s] = [cross(kept[s], -s, 0)] + [cross(sent[k - 1][s], -s, k) for k in range(1, n_tp)]
        else:
            if small and s == 0:
                sent[0][0], *_ = lax.optimization_barrier((sent[0][0], totals[2], totals[3]))
            come = [turn(sent[k - 1][s], "tp", k) for k in range(1, n_tp)]
            totals[s] = add([kept[s]] + come)
            home[s] = [turn(totals[s], "pool", -s) if s else totals[s]]
    layout, parts = [], []
    for s in range(n_pool):
        layout.append((len(home[s]), 0))
        parts += home[s]
    for u in range(1, n_pair):
        for s in range(n_pool):
            part = add([h[u * CAP : (u + 1) * CAP] for h in home[s]])
            layout.append((1, 0))
            parts.append(turn(part, "pair", u))
    (out,) = call(
        functools.partial(mix_kernel, n_pool, n_pair, layout),
        "mix",
        [shape(streams, width)],
        [VMEM] * (1 + len(parts)),
        (mixing, *parts),
        2 * 3 * streams * width,
    )
    return out


def solution(mesh):
    in_specs = (
        P(("groups", "pool", "pair"), "tp"),
        P(("groups", "pool", "pair"), None),
        P(("groups", "pool", "pair"), None),
        P(("pool", "pair"), None, "tp"),
        P(("pool", "pair"), None, "tp"),
        P(("pool", "pair"), "tp", None),
    )
    out_specs = P(("groups", "pool", "pair"), "tp")
    return jax.shard_map(body, mesh=mesh, in_specs=in_specs, out_specs=out_specs, check_vma=False)
```

```python
import functools

import jax
import jax.numpy as jnp
from jax import lax
from jax.experimental import pallas as pl
from jax.experimental.pallas import tpu as pltpu
from jax.sharding import PartitionSpec as P

CAP = 16
VMEM = pl.BlockSpec(memory_space=pltpu.VMEM)
SMEM = pl.BlockSpec(memory_space=pltpu.SMEM)
HBM = pl.BlockSpec(memory_space=pltpu.HBM)
BF16, F32 = jnp.bfloat16, jnp.float32


def call(kernel, name, outs, in_specs, args, nbytes, flops=0, scratch=(), alias=None, vmem=24, to=VMEM):
    return pl.pallas_call(
        kernel,
        out_shape=outs,
        in_specs=in_specs,
        out_specs=[to] * len(outs),
        scratch_shapes=scratch,
        input_output_aliases=alias or {},
        compiler_params=pltpu.CompilerParams(vmem_limit_bytes=vmem * 2**20),
        cost_estimate=pl.CostEstimate(flops=flops, bytes_accessed=nbytes, transcendentals=0),
        name=name,
    )(*args)


def picks(routes_t, experts):
    hits = [
        jnp.max((routes_t == e).astype(F32), axis=0, keepdims=True) for e in experts
    ]
    hits = jnp.concatenate(hits, axis=0)
    streams = hits.shape[1]
    earlier = lax.broadcasted_iota(jnp.int32, (streams, streams), 0)
    later = lax.broadcasted_iota(jnp.int32, (streams, streams), 1)
    before = (earlier < later).astype(BF16)
    slots = jnp.dot(hits.astype(BF16), before, preferred_element_type=F32)
    return hits, slots


def one_hot(hits, slots, row):
    streams = hits.shape[1]
    slot = lax.broadcasted_iota(jnp.int32, (CAP, streams), 0).astype(F32)
    return jnp.where((slots[row : row + 1] == slot) & (hits[row : row + 1] > 0), 1.0, 0.0)


def select(pos_ref, routes, tokens, outs, n_pool, n_pair, u, copy=None):
    pool, pair = pos_ref[0], pos_ref[1]
    experts = [lax.rem(pool + s, n_pool) * n_pair + pair for s in range(n_pool)]
    hits, slots = picks(routes[...], experts)
    sel = jnp.concatenate([one_hot(hits, slots, s) for s in range(n_pool)], axis=0)
    if copy is not None:
        copy.wait()
    rows = jnp.dot(sel.astype(BF16), tokens[...], preferred_element_type=F32).astype(BF16)
    for s in range(n_pool):
        outs[s][u * CAP : (u + 1) * CAP, :] = rows[s * CAP : (s + 1) * CAP]


def select_own_kernel(n_pool, n_pair, pos_ref, routes, tokens, *refs):
    outs, held, held_routes, sems = refs[:n_pool], refs[n_pool], refs[n_pool + 1], refs[n_pool + 2]
    first = pltpu.make_async_copy(routes, held_routes, sems.at[0])
    second = pltpu.make_async_copy(tokens, held, sems.at[1])
    first.start()
    second.start()
    first.wait()
    select(pos_ref, held_routes, held, outs, n_pool, n_pair, 0, second)


def select_other_kernel(n_pool, n_pair, pos_ref, *refs):
    others = n_pair - 1
    routes, tokens = refs[:others], refs[others : 2 * others]
    outs = refs[2 * others + n_pool :]
    held = refs[2 * others : 2 * others + n_pool]
    for s in range(n_pool):
        outs[s][:CAP, :] = held[s][:CAP, :]
    for u in range(1, n_pair):
        select(pos_ref, routes[u - 1], tokens[u - 1], outs, n_pool, n_pair, u)


def mixing_kernel(n_pool, n_pair, pos_ref, after_ref, routes_ref, weights_ref, out_ref):
    pool, pair = pos_ref[0], pos_ref[1]
    routes, weights = routes_ref[...], weights_ref[...]
    totals = jnp.sum(weights.astype(F32), axis=0, keepdims=True)
    experts = [
        lax.rem(pool + s, n_pool) * n_pair + lax.rem(pair - u + n_pair, n_pair)
        for u in range(n_pair)
        for s in range(n_pool)
    ]
    hits, slots = picks(routes, experts)
    mixing = []
    for i, e in enumerate(experts):
        chosen = jnp.where(routes == e, weights, 0).astype(F32)
        share = jnp.sum(chosen, axis=0, keepdims=True) / totals
        mixing.append(one_hot(hits, slots, i) * share)
    mixing = jnp.concatenate(mixing, axis=0).T
    n = mixing.shape[1]
    hi = mixing.astype(BF16)
    out_ref[:, :n] = hi
    out_ref[:, n:] = (mixing - hi.astype(F32)).astype(BF16)


def stacked(refs):
    return jnp.concatenate([r[...] for r in refs], axis=0)


def near_kernel(n_tp, tiles, pos_ref, gate_ref, up_ref, *refs):
    rows = refs[:-7]
    gate_out, up_out, gate_far, up_far, gate_near, up_near, sems = refs[-7:]
    width = rows[0].shape[1]
    tp = pos_ref[2]
    depth = width // tiles
    pairs = ((gate_ref, gate_near, gate_far), (up_ref, up_near, up_far))
    near, far = [], []
    for i in range(tiles):
        at = pl.ds(pl.multiple_of(tp * width + i * depth, depth), depth)
        for j, (ref, held, _) in enumerate(pairs):
            near.append(pltpu.make_async_copy(ref.at[at, :], held.at[pl.ds(i * depth, depth), :], sems.at[i * 2 + j]))
    for k in range(1, n_tp):
        for i in range(2):
            half = width // 2
            at = pl.ds(pl.multiple_of(lax.rem(tp - k + n_tp, n_tp) * width + i * half, half), half)
            to = pl.ds((k - 1) * width + i * half, half)
            for j, (ref, _, out) in enumerate(pairs):
                sem = sems.at[2 * tiles + ((k - 1) * 2 + i) * 2 + j]
                far.append(pltpu.make_async_copy(ref.at[at, :], out.at[to, :], sem))
    for c in near + far:
        c.start()
    block = stacked(rows)
    gate = up = None
    for i in range(tiles):
        cut = block[:, i * depth : (i + 1) * depth]
        near[2 * i].wait()
        g = jnp.dot(cut, gate_near[i * depth : (i + 1) * depth, :], preferred_element_type=F32)
        near[2 * i + 1].wait()
        u = jnp.dot(cut, up_near[i * depth : (i + 1) * depth, :], preferred_element_type=F32)
        gate, up = (g, u) if gate is None else (gate + g, up + u)
    gate_out[...] = gate
    up_out[...] = up
    for c in far:
        c.wait()


def far_kernel(n_tp, n_chunks, pos_ref, gate_ref, up_ref, down_ref, gate_in, up_in, *refs):
    far = n_tp - 1
    rows = [refs[k * n_chunks : (k + 1) * n_chunks] for k in range(far)]
    hidden_ref, outs = refs[far * n_chunks], refs[far * n_chunks + 1 :]
    width = down_ref.shape[1] // n_tp
    tp = pos_ref[2]
    gate, up = gate_in[...], up_in[...]
    for k in range(1, n_tp):
        at = pl.ds((k - 1) * width, width)
        block = stacked(rows[k - 1])
        gate += jnp.dot(block, gate_ref[at, :], preferred_element_type=F32)
        up += jnp.dot(block, up_ref[at, :], preferred_element_type=F32)
    hidden = (gate / (1.0 + jnp.exp(-gate)) * up).astype(BF16)
    hidden_ref[...] = hidden
    for k in range(1, n_tp):
        at = pl.ds(pl.multiple_of(lax.rem(tp + k, n_tp) * width, width), width)
        part = jnp.dot(hidden, down_ref[:, at], preferred_element_type=F32).astype(BF16)
        put(outs[(k - 1) * n_chunks : k * n_chunks], part)


def put(outs, part):
    at = 0
    for o in outs:
        o[...] = part[at : at + o.shape[0]]
        at += o.shape[0]


def keep_kernel(n_tp, pos_ref, down_ref, hidden_ref, *outs):
    width = outs[0].shape[1]
    at = pl.ds(pl.multiple_of(pos_ref[2] * width, width), width)
    put(outs, jnp.dot(hidden_ref[...], down_ref[:, at], preferred_element_type=F32).astype(BF16))


def mix_kernel(tiles, mixing_ref, *refs):
    parts, out, held, sems = refs[:-3], refs[-3], refs[-2], refs[-1]
    half = mixing_ref.shape[1] // 2
    high, low = mixing_ref[:, :half], mixing_ref[:, half:]
    cut = held.shape[1] // tiles
    copies = []
    for j in range(tiles):
        at = slice(j * cut, (j + 1) * cut)
        rows = jnp.concatenate([r[:CAP, at] for r in parts], axis=0)
        total = jnp.dot(high, rows, preferred_element_type=F32)
        total += jnp.dot(low, rows, preferred_element_type=F32)
        held[:, at] = total.astype(BF16)
        copies.append(pltpu.make_async_copy(held.at[:, at], out.at[:, at], sems.at[j]))
        copies[-1].start()
    for c in copies:
        c.wait()


def turn(x, axis, shift):
    n = lax.axis_size(axis)
    return lax.ppermute(x, axis, [(i, (i + shift) % n) for i in range(n)])


def cross(x, shift, k):
    n, m = lax.axis_size("pool"), lax.axis_size("tp")
    pairs = [(i * m + j, (i + shift) % n * m + (j + k) % m) for i in range(n) for j in range(m)]
    return lax.ppermute(x, ("pool", "tp"), pairs)


def add(parts):
    total = parts[0].astype(F32)
    for p in parts[1:]:
        total += p.astype(F32)
    return total.astype(BF16)


def body(tokens, routes, gate_weights, w_gate, w_up, w_down):
    n_pool, n_tp, n_pair = (lax.axis_size(a) for a in ("pool", "tp", "pair"))
    streams, width = tokens.shape
    hidden_units = w_gate.shape[2]
    pos = jnp.stack([lax.axis_index(a) for a in ("pool", "pair", "tp")]).astype(jnp.int32)
    routes_t, weights_t = routes.T, gate_weights.T
    rows = n_pair * CAP
    small = n_pool == 4 and n_tp == 2
    direct = []

    def shape(r, c, t=BF16):
        return jax.ShapeDtypeStruct((r, c), t)

    far_tokens = [turn(tokens, "pair", -u) for u in range(1, n_pair)]
    far_routes = [turn(routes_t, "pair", -u) for u in range(1, n_pair)]
    leaving = call(
        functools.partial(select_own_kernel, n_pool, n_pair),
        "select_own",
        [shape(rows, width)] * n_pool,
        [SMEM, HBM, HBM],
        (pos, pltpu.with_memory_space_constraint(routes_t, pltpu.HBM), pltpu.with_memory_space_constraint(tokens, pltpu.HBM)),
        2 * 2 * streams * width,
        scratch=[
            pltpu.VMEM((streams, width), BF16),
            pltpu.VMEM(routes_t.shape, routes.dtype),
            pltpu.SemaphoreType.DMA((2,)),
        ],
    )
    leaving = call(
        functools.partial(select_other_kernel, n_pool, n_pair),
        "select_other",
        [shape(rows, width)] * n_pool,
        [SMEM] + [VMEM] * (2 * (n_pair - 1) + n_pool),
        (pos, *far_routes, *far_tokens, *leaving),
        2 * 2 * streams * width,
        alias={1 + 2 * (n_pair - 1) + s: s for s in range(n_pool)},
    )
    gate_mat, up_mat, down_mat = w_gate[0], w_up[0], w_down[0]
    slots = n_pool * rows
    (mixing,) = call(
        functools.partial(mixing_kernel, n_pool, n_pair),
        "mixing",
        [shape(streams, 2 * slots)],
        [SMEM, VMEM, VMEM, VMEM],
        (pos, leaving[0], routes_t, weights_t),
        4 * 10 * streams * slots,
    )

    near = [leaving[0]] * n_pool
    for s in [3, 2, 1] if small else range(1, n_pool):
        near[s] = turn(leaving[s], "pool", s)
    first = 3 if small else 0
    near[first], mixing = lax.optimization_barrier((near[first], mixing))
    far = [[turn(b, "tp", k) for b in near] for k in range(1, n_tp)]
    tiles = 4 if width % 1024 == 0 else 1
    rest = (n_tp - 1) * width
    gate, up, gate_far, up_far = call(
        functools.partial(near_kernel, n_tp, tiles),
        "near",
        [shape(slots, hidden_units, F32)] * 2 + [shape(rest, hidden_units)] * 2,
        [SMEM] + [HBM] * 2 + [VMEM] * n_pool,
        (pos, gate_mat, up_mat, *near),
        2 * 2 * (w_gate.size + w_up.size),
        4 * slots * width * hidden_units,
        scratch=[pltpu.VMEM((width, hidden_units), BF16)] * 2
        + [pltpu.SemaphoreType.DMA((2 * tiles + 4 * (n_tp - 1),))],
        vmem=48,
    )
    hidden, *sent = call(
        functools.partial(far_kernel, n_tp, n_pool),
        "far",
        [shape(slots, hidden_units)] + [shape(rows, width)] * (n_pool * (n_tp - 1)),
        [SMEM] + [VMEM] * (5 + n_pool * (n_tp - 1)),
        (pos, gate_far, up_far, down_mat, gate, up, *sum(far, [])),
        8 * width * hidden_units,
        6 * slots * width * hidden_units,
    )
    sent = [sent[k * n_pool : (k + 1) * n_pool] for k in range(n_tp - 1)]
    kept = call(
        functools.partial(keep_kernel, n_tp),
        "keep",
        [shape(rows, width)] * n_pool,
        [SMEM] + [VMEM] * 2,
        (pos, down_mat, hidden),
        2 * width * hidden_units,
        2 * slots * width * hidden_units,
    )

    if small:
        late = [0, 1, 3]
        held, kept = lax.optimization_barrier(([sent[0][s] for s in late], kept))
        for s, x in zip(late, held):
            sent[0][s] = x
    home = [None] * n_pool
    totals = [None] * n_pool
    for s in [2, 3, 1, 0] if small else range(n_pool):
        if s in direct:
            home[s] = [cross(kept[s], -s, 0)] + [cross(sent[k - 1][s], -s, k) for k in range(1, n_tp)]
        else:
            if small and s == 0:
                sent[0][0], *_ = lax.optimization_barrier((sent[0][0], totals[2], totals[3]))
            come = [turn(sent[k - 1][s], "tp", k) for k in range(1, n_tp)]
            totals[s] = add([kept[s]] + come)
            home[s] = turn(totals[s], "pool", -s) if s else totals[s]
    parts = [home[s] for s in range(n_pool)]
    for u in range(1, n_pair):
        parts += [turn(home[s][u * CAP : (u + 1) * CAP], "pair", u) for s in range(n_pool)]
    tiles = 4 if width % 512 == 0 else 1
    (out,) = call(
        functools.partial(mix_kernel, tiles),
        "mix",
        [shape(streams, width)],
        [VMEM] * (1 + len(parts)),
        (mixing, *parts),
        2 * 3 * streams * width,
        scratch=[pltpu.VMEM((streams, width), BF16), pltpu.SemaphoreType.DMA((tiles,))],
        to=HBM,
    )
    return out


def solution(mesh):
    in_specs = (
        P(("groups", "pool", "pair"), "tp"),
        P(("groups", "pool", "pair"), None),
        P(("groups", "pool", "pair"), None),
        P(("pool", "pair"), None, "tp"),
        P(("pool", "pair"), None, "tp"),
        P(("pool", "pair"), "tp", None),
    )
    out_specs = P(("groups", "pool", "pair"), "tp")
    return jax.shard_map(body, mesh=mesh, in_specs=in_specs, out_specs=out_specs, check_vma=False)
```

```python
import functools

import jax
import jax.numpy as jnp
from jax import lax
from jax.experimental import pallas as pl
from jax.experimental.pallas import tpu as pltpu
from jax.sharding import PartitionSpec as P

CAP = 16
VMEM = pl.BlockSpec(memory_space=pltpu.VMEM)
HBM = pl.BlockSpec(memory_space=pltpu.HBM)
BF16, F32 = jnp.bfloat16, jnp.float32


def call(kernel, name, outs, in_specs, args, nbytes, flops=0, scratch=(), alias=None, vmem=24, to=VMEM):
    return pl.pallas_call(
        kernel,
        out_shape=outs,
        in_specs=in_specs,
        out_specs=[to] * len(outs),
        scratch_shapes=scratch,
        input_output_aliases=alias or {},
        compiler_params=pltpu.CompilerParams(vmem_limit_bytes=vmem * 2**20),
        cost_estimate=pl.CostEstimate(flops=flops, bytes_accessed=nbytes, transcendentals=0),
        name=name,
    )(*args)


def picks(routes_t, experts):
    hits = [
        jnp.max((routes_t == e).astype(F32), axis=0, keepdims=True) for e in experts
    ]
    hits = jnp.concatenate(hits, axis=0)
    streams = hits.shape[1]
    earlier = lax.broadcasted_iota(jnp.int32, (streams, streams), 0)
    later = lax.broadcasted_iota(jnp.int32, (streams, streams), 1)
    before = (earlier < later).astype(BF16)
    slots = jnp.dot(hits.astype(BF16), before, preferred_element_type=F32)
    return hits, slots


def one_hot(hits, slots, row):
    streams = hits.shape[1]
    slot = lax.broadcasted_iota(jnp.int32, (CAP, streams), 0).astype(F32)
    return jnp.where((slots[row : row + 1] == slot) & (hits[row : row + 1] > 0), 1.0, 0.0)


def select(routes, tokens, outs, n_pool, n_pair, u, copy=None):
    pool, pair = lax.axis_index("pool"), lax.axis_index("pair")
    experts = [lax.rem(pool + s, n_pool) * n_pair + pair for s in range(n_pool)]
    hits, slots = picks(routes[...], experts)
    sel = jnp.concatenate([one_hot(hits, slots, s) for s in range(n_pool)], axis=0)
    if copy is not None:
        copy.wait()
    rows = jnp.dot(sel.astype(BF16), tokens[...], preferred_element_type=F32).astype(BF16)
    for s in range(n_pool):
        outs[s][u * CAP : (u + 1) * CAP, :] = rows[s * CAP : (s + 1) * CAP]


def select_own_kernel(n_pool, n_pair, routes, tokens, *refs):
    outs, held, held_routes, sems = refs[:n_pool], refs[n_pool], refs[n_pool + 1], refs[n_pool + 2]
    first = pltpu.make_async_copy(routes, held_routes, sems.at[0])
    second = pltpu.make_async_copy(tokens, held, sems.at[1])
    first.start()
    second.start()
    first.wait()
    select(held_routes, held, outs, n_pool, n_pair, 0, second)


def select_other_kernel(n_pool, n_pair, *refs):
    others = n_pair - 1
    routes, tokens = refs[:others], refs[others : 2 * others]
    outs = refs[2 * others + n_pool :]
    held = refs[2 * others : 2 * others + n_pool]
    for s in range(n_pool):
        outs[s][:CAP, :] = held[s][:CAP, :]
    for u in range(1, n_pair):
        select(routes[u - 1], tokens[u - 1], outs, n_pool, n_pair, u)


def mixing_kernel(n_pool, n_pair, after_ref, routes_ref, weights_ref, out_ref):
    pool, pair = lax.axis_index("pool"), lax.axis_index("pair")
    routes, weights = routes_ref[...], weights_ref[...]
    totals = jnp.sum(weights.astype(F32), axis=0, keepdims=True)
    experts = [
        lax.rem(pool + s, n_pool) * n_pair + lax.rem(pair - u + n_pair, n_pair)
        for u in range(n_pair)
        for s in range(n_pool)
    ]
    hits, slots = picks(routes, experts)
    mixing = []
    for i, e in enumerate(experts):
        chosen = jnp.where(routes == e, weights, 0).astype(F32)
        share = jnp.sum(chosen, axis=0, keepdims=True) / totals
        mixing.append(one_hot(hits, slots, i) * share)
    mixing = jnp.concatenate(mixing, axis=0).T
    n = mixing.shape[1]
    hi = mixing.astype(BF16)
    out_ref[:, :n] = hi
    out_ref[:, n:] = (mixing - hi.astype(F32)).astype(BF16)


def stacked(refs):
    return jnp.concatenate([r[...] for r in refs], axis=0)


def near_kernel(n_tp, tiles, gate_ref, up_ref, *refs):
    rows = refs[:-7]
    gate_out, up_out, gate_far, up_far, gate_near, up_near, sems = refs[-7:]
    width = rows[0].shape[1]
    tp = lax.axis_index("tp")
    depth = width // tiles
    pairs = ((gate_ref, gate_near, gate_far), (up_ref, up_near, up_far))
    near, far = [], []
    for i in range(tiles):
        at = pl.ds(pl.multiple_of(tp * width + i * depth, depth), depth)
        for j, (ref, held, _) in enumerate(pairs):
            near.append(pltpu.make_async_copy(ref.at[at, :], held.at[pl.ds(i * depth, depth), :], sems.at[i * 2 + j]))
    for k in range(1, n_tp):
        for i in range(2):
            half = width // 2
            at = pl.ds(pl.multiple_of(lax.rem(tp - k + n_tp, n_tp) * width + i * half, half), half)
            to = pl.ds((k - 1) * width + i * half, half)
            for j, (ref, _, out) in enumerate(pairs):
                sem = sems.at[2 * tiles + ((k - 1) * 2 + i) * 2 + j]
                far.append(pltpu.make_async_copy(ref.at[at, :], out.at[to, :], sem))
    for c in near + far:
        c.start()
    block = stacked(rows)
    gate = up = None
    for i in range(tiles):
        cut = block[:, i * depth : (i + 1) * depth]
        near[2 * i].wait()
        g = jnp.dot(cut, gate_near[i * depth : (i + 1) * depth, :], preferred_element_type=F32)
        near[2 * i + 1].wait()
        u = jnp.dot(cut, up_near[i * depth : (i + 1) * depth, :], preferred_element_type=F32)
        gate, up = (g, u) if gate is None else (gate + g, up + u)
    gate_out[...] = gate
    up_out[...] = up
    for c in far:
        c.wait()


def far_kernel(n_tp, n_chunks, gate_ref, up_ref, down_ref, gate_in, up_in, *refs):
    far = n_tp - 1
    rows = [refs[k * n_chunks : (k + 1) * n_chunks] for k in range(far)]
    hidden_ref, outs = refs[far * n_chunks], refs[far * n_chunks + 1 :]
    width = down_ref.shape[1] // n_tp
    tp = lax.axis_index("tp")
    gate, up = gate_in[...], up_in[...]
    for k in range(1, n_tp):
        at = pl.ds((k - 1) * width, width)
        block = stacked(rows[k - 1])
        gate += jnp.dot(block, gate_ref[at, :], preferred_element_type=F32)
        up += jnp.dot(block, up_ref[at, :], preferred_element_type=F32)
    hidden = (gate / (1.0 + jnp.exp(-gate)) * up).astype(BF16)
    hidden_ref[...] = hidden
    for k in range(1, n_tp):
        at = pl.ds(pl.multiple_of(lax.rem(tp + k, n_tp) * width, width), width)
        part = jnp.dot(hidden, down_ref[:, at], preferred_element_type=F32).astype(BF16)
        put(outs[(k - 1) * n_chunks : k * n_chunks], part)


def put(outs, part):
    at = 0
    for o in outs:
        o[...] = part[at : at + o.shape[0]]
        at += o.shape[0]


def keep_kernel(n_tp, down_ref, hidden_ref, *outs):
    width = outs[0].shape[1]
    at = pl.ds(pl.multiple_of(lax.axis_index("tp") * width, width), width)
    put(outs, jnp.dot(hidden_ref[...], down_ref[:, at], preferred_element_type=F32).astype(BF16))


def mix_kernel(tiles, mixing_ref, *refs):
    parts, out, held, sems = refs[:-3], refs[-3], refs[-2], refs[-1]
    half = mixing_ref.shape[1] // 2
    high, low = mixing_ref[:, :half], mixing_ref[:, half:]
    cut = held.shape[1] // tiles
    copies = []
    for j in range(tiles):
        at = slice(j * cut, (j + 1) * cut)
        rows = jnp.concatenate([r[:CAP, at] for r in parts], axis=0)
        total = jnp.dot(high, rows, preferred_element_type=F32)
        total += jnp.dot(low, rows, preferred_element_type=F32)
        held[:, at] = total.astype(BF16)
        copies.append(pltpu.make_async_copy(held.at[:, at], out.at[:, at], sems.at[j]))
        copies[-1].start()
    for c in copies:
        c.wait()


def turn(x, axis, shift):
    n = lax.axis_size(axis)
    return lax.ppermute(x, axis, [(i, (i + shift) % n) for i in range(n)])


def cross(x, shift, k):
    n, m = lax.axis_size("pool"), lax.axis_size("tp")
    pairs = [(i * m + j, (i + shift) % n * m + (j + k) % m) for i in range(n) for j in range(m)]
    return lax.ppermute(x, ("pool", "tp"), pairs)


def add(parts):
    total = parts[0].astype(F32)
    for p in parts[1:]:
        total += p.astype(F32)
    return total.astype(BF16)


def body(tokens, routes, gate_weights, w_gate, w_up, w_down):
    n_pool, n_tp, n_pair = (lax.axis_size(a) for a in ("pool", "tp", "pair"))
    streams, width = tokens.shape
    hidden_units = w_gate.shape[2]
    routes_t, weights_t = routes.T, gate_weights.T
    rows = n_pair * CAP
    small = n_pool == 4 and n_tp == 2
    direct = []

    def shape(r, c, t=BF16):
        return jax.ShapeDtypeStruct((r, c), t)

    far_tokens = [turn(tokens, "pair", -u) for u in range(1, n_pair)]
    far_routes = [turn(routes_t, "pair", -u) for u in range(1, n_pair)]
    leaving = call(
        functools.partial(select_own_kernel, n_pool, n_pair),
        "select_own",
        [shape(rows, width)] * n_pool,
        [HBM, HBM],
        (pltpu.with_memory_space_constraint(routes_t, pltpu.HBM), pltpu.with_memory_space_constraint(tokens, pltpu.HBM)),
        2 * 2 * streams * width,
        scratch=[
            pltpu.VMEM((streams, width), BF16),
            pltpu.VMEM(routes_t.shape, routes.dtype),
            pltpu.SemaphoreType.DMA((2,)),
        ],
    )
    leaving = call(
        functools.partial(select_other_kernel, n_pool, n_pair),
        "select_other",
        [shape(rows, width)] * n_pool,
        [VMEM] * (2 * (n_pair - 1) + n_pool),
        (*far_routes, *far_tokens, *leaving),
        2 * 2 * streams * width,
        alias={2 * (n_pair - 1) + s: s for s in range(n_pool)},
    )
    gate_mat, up_mat, down_mat = w_gate[0], w_up[0], w_down[0]
    slots = n_pool * rows
    (mixing,) = call(
        functools.partial(mixing_kernel, n_pool, n_pair),
        "mixing",
        [shape(streams, 2 * slots)],
        [VMEM, VMEM, VMEM],
        (leaving[0], routes_t, weights_t),
        4 * 10 * streams * slots,
    )

    near = [leaving[0]] * n_pool
    for s in [3, 2, 1] if small else range(1, n_pool):
        near[s] = turn(leaving[s], "pool", s)
    first = 3 if small else 0
    near[first], mixing = lax.optimization_barrier((near[first], mixing))
    far = [[turn(b, "tp", k) for b in near] for k in range(1, n_tp)]
    tiles = 4 if width % 1024 == 0 else 1
    rest = (n_tp - 1) * width
    gate, up, gate_far, up_far = call(
        functools.partial(near_kernel, n_tp, tiles),
        "near",
        [shape(slots, hidden_units, F32)] * 2 + [shape(rest, hidden_units)] * 2,
        [HBM] * 2 + [VMEM] * n_pool,
        (gate_mat, up_mat, *near),
        2 * 2 * (w_gate.size + w_up.size),
        4 * slots * width * hidden_units,
        scratch=[pltpu.VMEM((width, hidden_units), BF16)] * 2
        + [pltpu.SemaphoreType.DMA((2 * tiles + 4 * (n_tp - 1),))],
        vmem=48,
    )
    hidden, *sent = call(
        functools.partial(far_kernel, n_tp, n_pool),
        "far",
        [shape(slots, hidden_units)] + [shape(rows, width)] * (n_pool * (n_tp - 1)),
        [VMEM] * (5 + n_pool * (n_tp - 1)),
        (gate_far, up_far, down_mat, gate, up, *sum(far, [])),
        8 * width * hidden_units,
        6 * slots * width * hidden_units,
    )
    sent = [sent[k * n_pool : (k + 1) * n_pool] for k in range(n_tp - 1)]
    kept = call(
        functools.partial(keep_kernel, n_tp),
        "keep",
        [shape(rows, width)] * n_pool,
        [VMEM] * 2,
        (down_mat, hidden),
        2 * width * hidden_units,
        2 * slots * width * hidden_units,
    )

    if small:
        late = [0, 1, 3]
        held, kept = lax.optimization_barrier(([sent[0][s] for s in late], kept))
        for s, x in zip(late, held):
            sent[0][s] = x
    home = [None] * n_pool
    totals = [None] * n_pool
    for s in [2, 3, 1, 0] if small else range(n_pool):
        if s in direct:
            home[s] = [cross(kept[s], -s, 0)] + [cross(sent[k - 1][s], -s, k) for k in range(1, n_tp)]
        else:
            if small and s == 0:
                sent[0][0], *_ = lax.optimization_barrier((sent[0][0], totals[2], totals[3]))
            come = [turn(sent[k - 1][s], "tp", k) for k in range(1, n_tp)]
            totals[s] = add([kept[s]] + come)
            home[s] = turn(totals[s], "pool", -s) if s else totals[s]
    parts = [home[s] for s in range(n_pool)]
    for u in range(1, n_pair):
        parts += [turn(home[s][u * CAP : (u + 1) * CAP], "pair", u) for s in range(n_pool)]
    tiles = 4 if width % 512 == 0 else 1
    (out,) = call(
        functools.partial(mix_kernel, tiles),
        "mix",
        [shape(streams, width)],
        [VMEM] * (1 + len(parts)),
        (mixing, *parts),
        2 * 3 * streams * width,
        scratch=[pltpu.VMEM((streams, width), BF16), pltpu.SemaphoreType.DMA((tiles,))],
        to=HBM,
    )
    return out


def solution(mesh):
    in_specs = (
        P(("groups", "pool", "pair"), "tp"),
        P(("groups", "pool", "pair"), None),
        P(("groups", "pool", "pair"), None),
        P(("pool", "pair"), None, "tp"),
        P(("pool", "pair"), None, "tp"),
        P(("pool", "pair"), "tp", None),
    )
    out_specs = P(("groups", "pool", "pair"), "tp")
    return jax.shard_map(body, mesh=mesh, in_specs=in_specs, out_specs=out_specs, check_vma=False)
```

```python
import functools

import jax
import jax.numpy as jnp
from jax import lax
from jax.experimental import pallas as pl
from jax.experimental.pallas import tpu as pltpu
from jax.sharding import PartitionSpec as P

CAP = 16
VMEM = pl.BlockSpec(memory_space=pltpu.VMEM)
HBM = pl.BlockSpec(memory_space=pltpu.HBM)
BF16, F32 = jnp.bfloat16, jnp.float32


def call(kernel, name, outs, in_specs, args, nbytes, flops=0, scratch=(), alias=None, vmem=24, to=VMEM):
    return pl.pallas_call(
        kernel,
        out_shape=outs,
        in_specs=in_specs,
        out_specs=[to] * len(outs),
        scratch_shapes=scratch,
        input_output_aliases=alias or {},
        compiler_params=pltpu.CompilerParams(vmem_limit_bytes=vmem * 2**20),
        cost_estimate=pl.CostEstimate(flops=flops, bytes_accessed=nbytes, transcendentals=0),
        name=name,
    )(*args)


def picks(routes_t, experts):
    hits = [
        jnp.max((routes_t == e).astype(F32), axis=0, keepdims=True) for e in experts
    ]
    hits = jnp.concatenate(hits, axis=0)
    streams = hits.shape[1]
    earlier = lax.broadcasted_iota(jnp.int32, (streams, streams), 0)
    later = lax.broadcasted_iota(jnp.int32, (streams, streams), 1)
    before = (earlier < later).astype(BF16)
    slots = jnp.dot(hits.astype(BF16), before, preferred_element_type=F32)
    return hits, slots


def one_hot(hits, slots, row):
    streams = hits.shape[1]
    slot = lax.broadcasted_iota(jnp.int32, (CAP, streams), 0).astype(F32)
    return jnp.where((slots[row : row + 1] == slot) & (hits[row : row + 1] > 0), 1.0, 0.0)


def select(routes, tokens, outs, n_pool, n_pair, u, copy=None):
    pool, pair = lax.axis_index("pool"), lax.axis_index("pair")
    experts = [lax.rem(pool + s, n_pool) * n_pair + pair for s in range(n_pool)]
    hits, slots = picks(routes[...], experts)
    sel = jnp.concatenate([one_hot(hits, slots, s) for s in range(n_pool)], axis=0)
    if copy is not None:
        copy.wait()
    rows = jnp.dot(sel.astype(BF16), tokens[...], preferred_element_type=F32).astype(BF16)
    for s in range(n_pool):
        outs[s][u * CAP : (u + 1) * CAP, :] = rows[s * CAP : (s + 1) * CAP]


def select_own_kernel(n_pool, n_pair, routes, weights, tokens, *refs):
    outs, held_routes, held_weights, held, sems = refs[:n_pool], *refs[n_pool:]
    first = pltpu.make_async_copy(routes, held_routes, sems.at[0])
    second = pltpu.make_async_copy(tokens, held, sems.at[1])
    third = pltpu.make_async_copy(weights, held_weights, sems.at[2])
    first.start()
    second.start()
    third.start()
    first.wait()
    select(held_routes, held, outs, n_pool, n_pair, 0, second)
    third.wait()


def select_other_kernel(n_pool, n_pair, *refs):
    others = n_pair - 1
    routes, tokens = refs[:others], refs[others : 2 * others]
    outs = refs[2 * others + n_pool :]
    held = refs[2 * others : 2 * others + n_pool]
    for s in range(n_pool):
        outs[s][:CAP, :] = held[s][:CAP, :]
    for u in range(1, n_pair):
        select(routes[u - 1], tokens[u - 1], outs, n_pool, n_pair, u)


def mixing_kernel(n_pool, n_pair, after_ref, routes_ref, weights_ref, out_ref):
    pool, pair = lax.axis_index("pool"), lax.axis_index("pair")
    routes, weights = routes_ref[...], weights_ref[...]
    totals = jnp.sum(weights.astype(F32), axis=0, keepdims=True)
    experts = [
        lax.rem(pool + s, n_pool) * n_pair + lax.rem(pair - u + n_pair, n_pair)
        for u in range(n_pair)
        for s in range(n_pool)
    ]
    hits, slots = picks(routes, experts)
    mixing = []
    for i, e in enumerate(experts):
        chosen = jnp.where(routes == e, weights, 0).astype(F32)
        share = jnp.sum(chosen, axis=0, keepdims=True) / totals
        mixing.append(one_hot(hits, slots, i) * share)
    mixing = jnp.concatenate(mixing, axis=0).T
    n = mixing.shape[1]
    hi = mixing.astype(BF16)
    out_ref[:, :n] = hi
    out_ref[:, n:] = (mixing - hi.astype(F32)).astype(BF16)


def stacked(refs):
    return jnp.concatenate([r[...] for r in refs], axis=0)


def near_kernel(n_tp, tiles, gate_ref, up_ref, down_ref, *refs):
    rows = refs[:-8]
    gate_out, up_out, gate_far, up_far, down_out, gate_near, up_near, sems = refs[-8:]
    width = rows[0].shape[1]
    tp = lax.axis_index("tp")
    depth = width // tiles
    pairs = ((gate_ref, gate_near, gate_far), (up_ref, up_near, up_far))
    near, far = [], []
    for i in range(tiles):
        at = pl.ds(pl.multiple_of(tp * width + i * depth, depth), depth)
        for j, (ref, held, _) in enumerate(pairs):
            near.append(pltpu.make_async_copy(ref.at[at, :], held.at[pl.ds(i * depth, depth), :], sems.at[i * 2 + j]))
    for k in range(1, n_tp):
        for i in range(2):
            half = width // 2
            at = pl.ds(pl.multiple_of(lax.rem(tp - k + n_tp, n_tp) * width + i * half, half), half)
            to = pl.ds((k - 1) * width + i * half, half)
            for j, (ref, _, out) in enumerate(pairs):
                sem = sems.at[2 * tiles + ((k - 1) * 2 + i) * 2 + j]
                far.append(pltpu.make_async_copy(ref.at[at, :], out.at[to, :], sem))
    for k in range(1, n_tp):
        at = pl.ds(pl.multiple_of(lax.rem(tp + k, n_tp) * width, width), width)
        to = pl.ds((k - 1) * width, width)
        sem = sems.at[2 * tiles + 4 * (n_tp - 1) + k - 1]
        far.append(pltpu.make_async_copy(down_ref.at[:, at], down_out.at[:, to], sem))
    for c in near + far:
        c.start()
    block = stacked(rows)
    gate = up = None
    for i in range(tiles):
        cut = block[:, i * depth : (i + 1) * depth]
        near[2 * i].wait()
        g = jnp.dot(cut, gate_near[i * depth : (i + 1) * depth, :], preferred_element_type=F32)
        near[2 * i + 1].wait()
        u = jnp.dot(cut, up_near[i * depth : (i + 1) * depth, :], preferred_element_type=F32)
        gate, up = (g, u) if gate is None else (gate + g, up + u)
    gate_out[...] = gate
    up_out[...] = up
    for c in far:
        c.wait()


def far_kernel(n_tp, n_chunks, gate_ref, up_ref, down_ref, gate_in, up_in, *refs):
    far = n_tp - 1
    rows = [refs[k * n_chunks : (k + 1) * n_chunks] for k in range(far)]
    hidden_ref, outs = refs[far * n_chunks], refs[far * n_chunks + 1 :]
    width = down_ref.shape[1] // far
    gate, up = gate_in[...], up_in[...]
    for k in range(1, n_tp):
        at = pl.ds((k - 1) * width, width)
        block = stacked(rows[k - 1])
        gate += jnp.dot(block, gate_ref[at, :], preferred_element_type=F32)
        up += jnp.dot(block, up_ref[at, :], preferred_element_type=F32)
    hidden = (gate / (1.0 + jnp.exp(-gate)) * up).astype(BF16)
    hidden_ref[...] = hidden
    for k in range(1, n_tp):
        at = pl.ds((k - 1) * width, width)
        part = jnp.dot(hidden, down_ref[:, at], preferred_element_type=F32).astype(BF16)
        put(outs[(k - 1) * n_chunks : k * n_chunks], part)


def put(outs, part):
    at = 0
    for o in outs:
        o[...] = part[at : at + o.shape[0]]
        at += o.shape[0]


def keep_kernel(n_tp, down_ref, hidden_ref, *outs):
    width = outs[0].shape[1]
    at = pl.ds(pl.multiple_of(lax.axis_index("tp") * width, width), width)
    put(outs, jnp.dot(hidden_ref[...], down_ref[:, at], preferred_element_type=F32).astype(BF16))


def mix_kernel(tiles, mixing_ref, *refs):
    parts, out, held, sems = refs[:-3], refs[-3], refs[-2], refs[-1]
    half = mixing_ref.shape[1] // 2
    high, low = mixing_ref[:, :half], mixing_ref[:, half:]
    cut = held.shape[1] // tiles
    copies = []
    for j in range(tiles):
        at = slice(j * cut, (j + 1) * cut)
        rows = jnp.concatenate([r[:CAP, at] for r in parts], axis=0)
        total = jnp.dot(high, rows, preferred_element_type=F32)
        total += jnp.dot(low, rows, preferred_element_type=F32)
        held[:, at] = total.astype(BF16)
        copies.append(pltpu.make_async_copy(held.at[:, at], out.at[:, at], sems.at[j]))
        copies[-1].start()
    for c in copies:
        c.wait()


def turn(x, axis, shift):
    n = lax.axis_size(axis)
    return lax.ppermute(x, axis, [(i, (i + shift) % n) for i in range(n)])


def cross(x, shift, k):
    n, m = lax.axis_size("pool"), lax.axis_size("tp")
    pairs = [(i * m + j, (i + shift) % n * m + (j + k) % m) for i in range(n) for j in range(m)]
    return lax.ppermute(x, ("pool", "tp"), pairs)


def add(parts):
    total = parts[0].astype(F32)
    for p in parts[1:]:
        total += p.astype(F32)
    return total.astype(BF16)


def body(tokens, routes, gate_weights, w_gate, w_up, w_down):
    n_pool, n_tp, n_pair = (lax.axis_size(a) for a in ("pool", "tp", "pair"))
    streams, width = tokens.shape
    hidden_units = w_gate.shape[2]
    routes_t, weights_t = routes.T, gate_weights.T
    rows = n_pair * CAP
    small = n_pool == 4 and n_tp == 2
    direct = []

    def shape(r, c, t=BF16):
        return jax.ShapeDtypeStruct((r, c), t)

    far_tokens = [turn(tokens, "pair", -u) for u in range(1, n_pair)]
    far_routes = [turn(routes_t, "pair", -u) for u in range(1, n_pair)]
    *leaving, near_routes, near_weights = call(
        functools.partial(select_own_kernel, n_pool, n_pair),
        "select_own",
        [shape(rows, width)] * n_pool + [shape(*x.shape, x.dtype) for x in (routes_t, weights_t)],
        [HBM] * 3,
        [pltpu.with_memory_space_constraint(x, pltpu.HBM) for x in (routes_t, weights_t, tokens)],
        2 * 2 * streams * width,
        scratch=[pltpu.VMEM((streams, width), BF16), pltpu.SemaphoreType.DMA((3,))],
    )
    leaving = call(
        functools.partial(select_other_kernel, n_pool, n_pair),
        "select_other",
        [shape(rows, width)] * n_pool,
        [VMEM] * (2 * (n_pair - 1) + n_pool),
        (*far_routes, *far_tokens, *leaving),
        2 * 2 * streams * width,
        alias={2 * (n_pair - 1) + s: s for s in range(n_pool)},
    )
    gate_mat, up_mat, down_mat = w_gate[0], w_up[0], w_down[0]
    slots = n_pool * rows
    (mixing,) = call(
        functools.partial(mixing_kernel, n_pool, n_pair),
        "mixing",
        [shape(streams, 2 * slots)],
        [VMEM, VMEM, VMEM],
        (leaving[0], near_routes, near_weights),
        4 * 10 * streams * slots,
    )

    near = [leaving[0]] * n_pool
    for s in [3, 2, 1] if small else range(1, n_pool):
        near[s] = turn(leaving[s], "pool", s)
    first = 3 if small else 0
    near[first], mixing = lax.optimization_barrier((near[first], mixing))
    far = [[turn(b, "tp", k) for b in near] for k in range(1, n_tp)]
    tiles = 4 if width % 1024 == 0 else 1
    rest = (n_tp - 1) * width
    gate, up, gate_far, up_far, down_far = call(
        functools.partial(near_kernel, n_tp, tiles),
        "near",
        [shape(slots, hidden_units, F32)] * 2 + [shape(rest, hidden_units)] * 2 + [shape(hidden_units, rest)],
        [HBM] * 3 + [VMEM] * n_pool,
        (*[pltpu.with_memory_space_constraint(w, pltpu.HBM) for w in (gate_mat, up_mat, down_mat)], *near),
        2 * 2 * (w_gate.size + w_up.size),
        4 * slots * width * hidden_units,
        scratch=[pltpu.VMEM((width, hidden_units), BF16)] * 2
        + [pltpu.SemaphoreType.DMA((2 * tiles + 5 * (n_tp - 1),))],
        vmem=24,
    )
    hidden, *sent = call(
        functools.partial(far_kernel, n_tp, n_pool),
        "far",
        [shape(slots, hidden_units)] + [shape(rows, width)] * (n_pool * (n_tp - 1)),
        [VMEM] * (5 + n_pool * (n_tp - 1)),
        (gate_far, up_far, down_far, gate, up, *sum(far, [])),
        8 * width * hidden_units,
        6 * slots * width * hidden_units,
    )
    sent = [sent[k * n_pool : (k + 1) * n_pool] for k in range(n_tp - 1)]
    kept = call(
        functools.partial(keep_kernel, n_tp),
        "keep",
        [shape(rows, width)] * n_pool,
        [VMEM] * 2,
        (down_mat, hidden),
        2 * width * hidden_units,
        2 * slots * width * hidden_units,
    )

    if small:
        late = [0, 1, 3]
        held, kept = lax.optimization_barrier(([sent[0][s] for s in late], kept))
        for s, x in zip(late, held):
            sent[0][s] = x
    home = [None] * n_pool
    totals = [None] * n_pool
    for s in [2, 3, 1, 0] if small else range(n_pool):
        if s in direct:
            home[s] = [cross(kept[s], -s, 0)] + [cross(sent[k - 1][s], -s, k) for k in range(1, n_tp)]
        else:
            if small and s == 0:
                sent[0][0], *_ = lax.optimization_barrier((sent[0][0], totals[2], totals[3]))
            come = [turn(sent[k - 1][s], "tp", k) for k in range(1, n_tp)]
            totals[s] = add([kept[s]] + come)
            home[s] = turn(totals[s], "pool", -s) if s else totals[s]
    parts = [home[s] for s in range(n_pool)]
    for u in range(1, n_pair):
        parts += [turn(home[s][u * CAP : (u + 1) * CAP], "pair", u) for s in range(n_pool)]
    tiles = 4 if width % 512 == 0 else 1
    (out,) = call(
        functools.partial(mix_kernel, tiles),
        "mix",
        [shape(streams, width)],
        [VMEM] * (1 + len(parts)),
        (mixing, *parts),
        2 * 3 * streams * width,
        scratch=[pltpu.VMEM((streams, width), BF16), pltpu.SemaphoreType.DMA((tiles,))],
        to=HBM,
    )
    return out


def solution(mesh):
    in_specs = (
        P(("groups", "pool", "pair"), "tp"),
        P(("groups", "pool", "pair"), None),
        P(("groups", "pool", "pair"), None),
        P(("pool", "pair"), None, "tp"),
        P(("pool", "pair"), None, "tp"),
        P(("pool", "pair"), "tp", None),
    )
    out_specs = P(("groups", "pool", "pair"), "tp")
    return jax.shard_map(body, mesh=mesh, in_specs=in_specs, out_specs=out_specs, check_vma=False)
```
